1024 devices in a mesh: box: 64 (over z, core), sub: 16 (over y, x).
Axes of the slice: x: 4, y: 4, z: 32, core: 2. Of those that a mesh axis runs over, the one named last changes fastest.
Arguments:
- source: float32 [256, 512, 256], P('box', 'sub'), may hold values from -8 to 8
- guess: float32 [256, 512, 256], P('box', 'sub'), may hold values from -8 to 8
- mass_coef: float32 [256, 512, 256], P('box', 'sub'), may hold values from 0.05 to 1
- diffusion: float32 [256, 512, 256], P('box', 'sub'), may hold values from 0.25 to 4
Outputs:
- final: float32 [256, 512, 256], P('box', 'sub')
The draws below stay inside these ranges and needn't reach their ends.
All inputs are finite; a program needn't handle non-finite values.
Results may differ from the reference program's by a relative error of at most 0.00002.
Values sent between devices are 32-bit elements; how exact they have to be, the bound alone decides.
A program may use at most 32 MiB of HBM per device.

```python
import math
import jax
import jax.numpy as jnp
from jax import lax

CZ = 256
CHEB_C = 8
NX = 256
NY = 512


def levels(stream_key, shape, split, low, largest):
    def one(axis_at, parts):
        draws = jax.random.uniform(jax.random.fold_in(jax.random.fold_in(stream_key, 6), axis_at), (parts,), jnp.float32, low / len(split), largest / len(split))
        return jnp.repeat(jnp.exp(draws), shape[axis_at] // parts).reshape((-1,) + (1,) * (len(shape) - axis_at - 1))

    level = one(*split[0])
    for cut in split[1:]:
        level = level * one(*cut)
    return level


def gaussian(key, extent, spread, limit, cuts=(), kind=jnp.bfloat16):
    entries = spread * jax.random.normal(key, extent, jnp.float32)
    if cuts:
        entries = entries * levels(key, extent, cuts, -0.22, 0.18)
    return jnp.clip(entries, -limit, limit).astype(kind)


def setup_inputs(seed: int = 0) -> dict:
    arg_keys = jax.random.split(jax.random.key(seed), 5)
    return {
        "source": gaussian(arg_keys[0], (NX, NY, CZ), 1.0, 8.0, ((0, 64), (1, 16)), jnp.float32),
        "guess": gaussian(arg_keys[1], (NX, NY, CZ), 1.0, 8.0, ((0, 64), (1, 16)), jnp.float32),
        "mass_coef": jnp.clip(jnp.exp(math.log(1.0) - 2.9957323 * jax.random.uniform(arg_keys[2], (NX, NY, CZ), jnp.float32) ** levels(arg_keys[2], (NX, NY, CZ), ((0, 64), (1, 16)), -0.2, 0.2)), 0.05, 1.0),
        "diffusion": jnp.clip(jnp.exp(math.log(4.0) - 2.7725887 * jax.random.uniform(arg_keys[3], (NX, NY, CZ), jnp.float32) ** levels(arg_keys[3], (NX, NY, CZ), ((0, 64), (1, 16)), -0.2, 0.2)), 0.25, 4.0),
    }


FINE_LOW = 0.25
FINE_HIGH = 2.0
COARSE_LOW = 0.05
COARSE_HIGH = 2.0


def cheb_coeffs(count_steps, low_end, high_end):
    center_val = (high_end + low_end) / 2.0
    half_width = (high_end - low_end) / 2.0
    sigma_val = center_val / half_width
    factor_prev = 1.0 / sigma_val
    coeffs_list = [(0.0, 1.0 / center_val)]
    for number in range(1, count_steps):
        factor_next = 1.0 / (2.0 * sigma_val - factor_prev)
        coeffs_list.append((factor_next * factor_prev, 2.0 * factor_next / half_width))
        factor_prev = factor_next
    return coeffs_list


def halve_dims(array, dims):
    for axis_num in dims:
        array = 0.5 * (lax.slice_in_dim(array, 0, None, 2, axis_num) + lax.slice_in_dim(array, 1, None, 2, axis_num))
    return array


def fine_apply(field, mass, face_x, face_y, face_z):
    padded = jnp.pad(field, 1)
    diagonal = mass + face_x[:-1] + face_x[1:] + face_y[:, :-1] + face_y[:, 1:] + face_z[:, :, :-1] + face_z[:, :, 1:]
    neighbours = (face_x[:-1] * padded[:-2, 1:-1, 1:-1] + face_x[1:] * padded[2:, 1:-1, 1:-1]
                  + face_y[:, :-1] * padded[1:-1, :-2, 1:-1] + face_y[:, 1:] * padded[1:-1, 2:, 1:-1]
                  + face_z[:, :, :-1] * padded[1:-1, 1:-1, :-2] + face_z[:, :, 1:] * padded[1:-1, 1:-1, 2:])
    return diagonal * field - neighbours, diagonal


def coarse_apply(field, mass, lows, highs):
    padded = jnp.pad(field, 1)
    diagonal = mass + 0.25 * (lows[0] + highs[0] + lows[1] + highs[1] + lows[2] + highs[2])
    neighbours = (lows[0] * padded[:-2, 1:-1, 1:-1] + highs[0] * padded[2:, 1:-1, 1:-1]
                  + lows[1] * padded[1:-1, :-2, 1:-1] + highs[1] * padded[1:-1, 2:, 1:-1]
                  + lows[2] * padded[1:-1, 1:-1, :-2] + highs[2] * padded[1:-1, 1:-1, 2:])
    return diagonal * field - 0.25 * neighbours, diagonal


def chebyshev(start, rhs, operator, coeffs):
    field = start
    step_dir = jnp.zeros_like(start)
    for keep_part, gain_part in coeffs:
        applied, diagonal = operator(field)
        step_dir = keep_part * step_dir + gain_part * (rhs - applied) / diagonal
        field = field + step_dir
    return field


def reference(source, guess, mass_coef, diffusion):
    diff_padded = jnp.pad(diffusion, 1)
    face_x = 0.5 * (diff_padded[:-1, 1:-1, 1:-1] + diff_padded[1:, 1:-1, 1:-1])
    face_y = 0.5 * (diff_padded[1:-1, :-1, 1:-1] + diff_padded[1:-1, 1:, 1:-1])
    face_z = 0.5 * (diff_padded[1:-1, 1:-1, :-1] + diff_padded[1:-1, 1:-1, 1:])

    def fine_op(field):
        return fine_apply(field, mass_coef, face_x, face_y, face_z)

    fine_steps = cheb_coeffs(2, FINE_LOW, FINE_HIGH)
    smoothed = chebyshev(guess, source, fine_op, fine_steps)
    applied, unused = fine_op(smoothed)
    residual = source - applied
    coarse_rhs = halve_dims(residual, (0, 1, 2))
    coarse_mass = halve_dims(mass_coef, (0, 1, 2))
    lows = (halve_dims(face_x[:-1:2], (1, 2)), halve_dims(face_y[:, :-1:2], (0, 2)), halve_dims(face_z[:, :, :-1:2], (0, 1)))
    highs = (halve_dims(face_x[2::2], (1, 2)), halve_dims(face_y[:, 2::2], (0, 2)), halve_dims(face_z[:, :, 2::2], (0, 1)))

    def coarse_op(field):
        return coarse_apply(field, coarse_mass, lows, highs)

    correction = chebyshev(jnp.zeros_like(coarse_rhs), coarse_rhs, coarse_op, cheb_coeffs(CHEB_C, COARSE_LOW, COARSE_HIGH))
    prolonged = jnp.repeat(jnp.repeat(jnp.repeat(correction, 2, 0), 2, 1), 2, 2)
    final = chebyshev(smoothed + prolonged, source, fine_op, fine_steps)
    return final
```

```python
import functools

import jax
import jax.numpy as jnp
from jax import lax
from jax.experimental import pallas as pl
from jax.experimental.pallas import tpu as pltpu
from jax.sharding import PartitionSpec as P

MESH = pl.DeviceIdType.MESH
CHEB_C = 8
FINE_LOW = 0.25
FINE_HIGH = 2.0
COARSE_LOW = 0.05
COARSE_HIGH = 2.0

FX0, FX1, FR0, FRN = 3, 7, 4, 32
CX0, CR0, CRN = 4, 4, 16
GUESS, DIFF, SOURCE, MASS = 0, 1, 2, 3

NEAR = [(i, j) for i in (-2, 2, -1, 1) for j in (-1, 1)] + [(-2, 0), (2, 0), (0, -1), (0, 1), (-1, 0), (1, 0)]
RING = [(i, j) for i in (-1, 1) for j in (-1, 1)] + [(0, -1), (0, 1), (-1, 0), (1, 0)]


def cheb_coeffs(count_steps, low_end, high_end):
    center_val = (high_end + low_end) / 2.0
    half_width = (high_end - low_end) / 2.0
    sigma_val = center_val / half_width
    factor_prev = 1.0 / sigma_val
    coeffs_list = [(0.0, 1.0 / center_val)]
    for number in range(1, count_steps):
        factor_next = 1.0 / (2.0 * sigma_val - factor_prev)
        coeffs_list.append((factor_next * factor_prev, 2.0 * factor_next / half_width))
        factor_prev = factor_next
    return coeffs_list


def coarse_rows(os):
    if os == 1:
        return pl.ds(CR0 + CRN - 4, 4), pl.ds(0, 4)
    if os == -1:
        return pl.ds(CR0, 4), pl.ds(CR0 + CRN, 4)
    return pl.ds(CR0, CRN), pl.ds(CR0, CRN)


def fine_cut(o, start, size, width):
    if o == 1:
        return pl.ds(start + size - width, width), pl.ds(start - width, width)
    if o == -1:
        return pl.ds(start, width), pl.ds(start + size, width)
    return pl.ds(start, size), pl.ds(start, size)


def rim_messages():
    found = []
    for i in (-1, 1):
        found.append(((i, 0), pl.ds(0, 2), 3, FRN))
    for i in (-1, 1):
        for j in (-1, 1):
            found.append(((i, j), pl.ds(0, 4), 2, 2))
    for j in (-1, 1):
        found.append(((0, j), pl.ds(0, 4), 4, 3))
    for i in (-1, 1):
        found.append(((i, 0), pl.ds(2, 2), 2, FRN))
    return found


def dot(a, b):
    return jnp.dot(a, b, precision=lax.Precision.HIGHEST, preferred_element_type=jnp.float32)


def kernel(source, guess, mass, diff, out, F, FX, FY, FZ, DIAG, INV, W1, W2, DIR, RES, L2, C, G, A, B, XA, XB, CD,
           load_sem, r_send, r_recv, c_send, c_recv, e_send, e_recv, b_send, b_recv, l_send, l_recv):
    f32 = jnp.float32
    nbox, nsub = lax.axis_size("box"), lax.axis_size("sub")
    b, s = lax.axis_index("box"), lax.axis_index("sub")

    def device(o):
        return (lax.rem(b + o[0] + nbox, nbox), lax.rem(s + o[1] + nsub, nsub))

    loads = []
    for k, ref in enumerate((guess, diff, source, mass)):
        for h in range(2):
            loads.append(pltpu.make_async_copy(
                ref.at[:, :, pl.ds(128 * h, 128)], F.at[k, pl.ds(FX0, 4), h, pl.ds(FR0, FRN)], load_sem.at[k, h]))
            loads[-1].start()
    barrier = pltpu.get_barrier_semaphore()
    for o in NEAR:
        pl.semaphore_signal(barrier, inc=1, device_id=device(o), device_id_type=MESH)
    for load in loads:
        load.wait()
    pl.semaphore_wait(barrier, len(NEAR))

    first = []
    for k, (o, arrays, xw, rw) in enumerate(rim_messages()):
        xs, xd = fine_cut(o[0], FX0, 4, xw)
        rs, rd = fine_cut(o[1], FR0, FRN, rw)
        first.append(pltpu.make_async_remote_copy(
            src_ref=F.at[arrays, xs, :, rs], dst_ref=F.at[arrays, xd, :, rd],
            send_sem=r_send.at[k], recv_sem=r_recv.at[k], device_id=device(o), device_id_type=MESH))
        first[-1].start()

    lane = lax.broadcasted_iota(jnp.int32, (256, 128), 0)
    cell = lax.broadcasted_iota(jnp.int32, (256, 128), 1)
    z_mean = jnp.where(lax.shift_right_logical(lane, 1) == cell, f32(0.5), f32(0.0))
    z_low = jnp.where(lax.shift_right_logical(lane + 1, 1) == cell, f32(0.5), f32(0.0))
    z_high = jnp.where(lax.shift_right_logical(lane + 1, 1) == cell + 1, f32(0.5), f32(0.0))
    row = lax.broadcasted_iota(jnp.int32, (2, 40, 128), 1)
    row_in = jnp.logical_and(jnp.logical_or(row >= FR0, s > 0), jnp.logical_or(row < FR0 + FRN, s < nsub - 1))
    row_mask = jnp.where(row_in, f32(1.0), f32(0.0))
    lane_f = lax.broadcasted_iota(jnp.int32, (2, 40, 128), 2)
    half = lax.broadcasted_iota(jnp.int32, (2, 40, 128), 0)
    z_first = jnp.logical_and(lane_f == 0, half == 0)
    z_last = jnp.logical_and(lane_f == 127, half == 1)

    def shift(v, edge, by):
        r = pltpu.roll(v, by, 2)
        return jnp.where(edge, jnp.stack([r[1], r[0]]), r)

    def from_below(v):
        return shift(v, lane_f == 0, 1)

    def from_above(v):
        return shift(v, lane_f == 127, 127)


    def slab_in(x):
        inside = jnp.logical_and(jnp.logical_or(x >= FX0, b > 0), jnp.logical_or(x < FX1, b < nbox - 1))
        return jnp.where(inside, f32(1.0), f32(0.0))

    for message in first:
        message.wait_recv()

    @pl.when(b == 0)
    def _():
        F[0:2, 0:FX0] = jnp.zeros((2, FX0, 2, 40, 128), f32)

    @pl.when(b == nbox - 1)
    def _():
        F[0:2, FX1:10] = jnp.zeros((2, 10 - FX1, 2, 40, 128), f32)

    @pl.when(s == 0)
    def _():
        F[0:2, :, :, 0:FR0] = jnp.zeros((2, 10, 2, FR0, 128), f32)

    @pl.when(s == nsub - 1)
    def _():
        F[0:2, :, :, FR0 + FRN:40] = jnp.zeros((2, 10, 2, 40 - FR0 - FRN, 128), f32)

    def rows(ref, x, start):
        return ref[x, :, pl.ds(start, 16, 2), :]

    def wide(parts):
        return jnp.concatenate([jnp.concatenate([v[0], v[1]], 1) for v in parts], 0)


    D, M = F.at[DIFF], F.at[MASS]
    pair = {x: rows(D, x, FR0) + rows(D, x, FR0 + 1) for x in range(FX0 - 1, FX1 + 1)}
    low_y = {x: rows(D, x, FR0 - 1) + rows(D, x, FR0) for x in range(FX0, FX1)}
    high_y = {x: rows(D, x, FR0 + 1) + rows(D, x, FR0 + 2) for x in range(FX0, FX1)}
    in_mean, in_z = [], []
    for X in range(2):
        x = FX0 + 2 * X
        face_low, face_high = 0.25 * (pair[x - 1] + pair[x]), 0.25 * (pair[x + 1] + pair[x + 2])
        y_low, y_high = 0.25 * (low_y[x] + low_y[x + 1]), 0.25 * (high_y[x] + high_y[x + 1])
        mean_mass = 0.25 * (rows(M, x, FR0) + rows(M, x, FR0 + 1) + rows(M, x + 1, FR0) + rows(M, x + 1, FR0 + 1))
        in_mean += [face_low, y_low, mean_mass + 0.25 * (face_low + face_high + y_low + y_high)]
        in_z.append(0.25 * (pair[x] + pair[x + 1]))
    means = dot(wide(in_mean), z_mean)
    over_z = wide(in_z)
    lows_z, highs_z = dot(over_z, z_low), dot(over_z, z_high)
    own_s = []
    for X in range(2):
        fx, fy, d = (means[(3 * X + k) * 16:(3 * X + k + 1) * 16] for k in range(3))
        fz = lows_z[16 * X:16 * X + 16]
        d = d + 0.25 * (fz + highs_z[16 * X:16 * X + 16])
        sc = lax.rsqrt(d)
        sc = sc * (1.5 - 0.5 * d * sc * sc)
        own_s.append(sc)
        for k, v in enumerate((fx, fy, fz, sc)):
            C[k, CX0 + X, pl.ds(CR0, CRN), :] = v

    def coarse_messages(src, lead, sends, recvs):
        found = []
        for k, o in enumerate(NEAR):
            rs, rd = coarse_rows(o[1])
            at_src = lead + (pl.ds(CX0, 2), rs)
            at_dst = lead + (pl.ds(CX0 - 2 * o[0], 2), rd)
            found.append(pltpu.make_async_remote_copy(
                src_ref=src.at[at_src], dst_ref=src.at[at_dst],
                send_sem=sends.at[k], recv_sem=recvs.at[k], device_id=device(o), device_id_type=MESH))
            found[-1].start()
        return found

    coefs = coarse_messages(C, (pl.ds(0, 4),), c_send, c_recv)

    def face_body(x, carry):
        FX[x] = 0.5 * (F[DIFF, x - 1] + F[DIFF, x])
        return carry

    lax.fori_loop(1, 10, face_body, 0)

    def operator_body(x, carry):
        d = F[DIFF, x]
        fy = 0.5 * (d + pltpu.roll(d, 1, 1))
        fz = 0.5 * (d + jnp.where(z_first, f32(0.0), from_below(d)))
        fz_high = 0.5 * (d + jnp.where(z_last, f32(0.0), from_above(d)))
        diag = F[MASS, x] + FX[x] + FX[x + 1] + fy + pltpu.roll(fy, 39, 1) + fz + fz_high
        FY[x] = fy
        FZ[x] = jnp.where(z_first, f32(0.0), fz)
        DIAG[x] = diag
        INV[x] = (row_mask * slab_in(x)) / diag
        return carry

    lax.fori_loop(1, 9, operator_body, 0)

    def defect(u_ref, x):
        u = u_ref[x]
        fy, fz = FY[x], FZ[x]
        around = FX[x] * u_ref[x - 1] + FX[x + 1] * u_ref[x + 1]
        around = around + fy * pltpu.roll(u, 1, 1) + pltpu.roll(fy * u, 39, 1)
        around = around + fz * from_below(u) + from_above(fz * u)
        return (F[SOURCE, x] - DIAG[x] * u) + around, u

    fine = cheb_coeffs(2, FINE_LOW, FINE_HIGH)
    coarse = cheb_coeffs(CHEB_C, COARSE_LOW, COARSE_HIGH)

    def first_step(u_ref, to_ref):
        def body(x, carry):
            c, u = defect(u_ref, x)
            step_dir = (fine[0][1] * INV[x]) * c
            DIR[x] = step_dir
            to_ref[x] = u + step_dir
            return carry

        return body

    lax.fori_loop(1, 9, first_step(F.at[GUESS], W1), 0)

    def second_step(x):
        c, u = defect(W1, x)
        return u + (fine[1][0] * DIR[x] + (fine[1][1] * INV[x]) * c)

    def second_body(x, carry):
        W2[x] = second_step(x)
        return carry

    lax.fori_loop(2, 8, second_body, 0)

    def residual_body(x, carry):
        RES[x] = defect(W2, x)[0]
        return carry

    lax.fori_loop(FX0, FX1, residual_body, 0)

    means = []
    for X in range(2):
        x = FX0 + 2 * X
        means.append(0.25 * ((rows(RES, x, FR0) + rows(RES, x, FR0 + 1)) + (rows(RES, x + 1, FR0) + rows(RES, x + 1, FR0 + 1))))
    rhs = dot(wide(means), z_mean)
    for X in range(2):
        A[CX0 + X, pl.ds(CR0, CRN), :] = own_s[X] * rhs[16 * X:16 * X + 16]
    e_one = coarse_messages(A, (), e_send, e_recv)

    for x in range(FX0, FX1):
        L2[x, :, pl.ds(FR0, FRN), :] = W2[x, :, pl.ds(FR0, FRN), :]
    late = []
    for k, o in enumerate(RING):
        xs, xd = fine_cut(o[0], FX0, 4, 2)
        rs, rd = fine_cut(o[1], FR0, FRN, 2)
        late.append(pltpu.make_async_remote_copy(
            src_ref=L2.at[xs, :, rs], dst_ref=L2.at[xd, :, rd],
            send_sem=l_send.at[k], recv_sem=l_recv.at[k], device_id=device(o), device_id_type=MESH))
        late[-1].start()

    for message in coefs:
        message.wait_recv()
    crow = lax.broadcasted_iota(jnp.int32, (24, 128), 0)
    clane = lax.broadcasted_iota(jnp.int32, (24, 128), 1)
    first_row = jnp.logical_or(jnp.logical_and(s == 0, crow == CR0), jnp.logical_and(s == nsub - 1, crow == CR0 + CRN))
    for X in range(10):
        sc = C[3, X]
        if X > 0:
            edge = lax.rem(2 * b + (X - CX0) + 2 * nbox, 2 * nbox) == 0
            G[0, X] = C[0, X] * ((0.25 * sc) * C[3, X - 1]) * jnp.where(edge, f32(0.0), f32(1.0))
        G[1, X] = jnp.where(first_row, f32(0.0), C[1, X] * ((0.25 * sc) * pltpu.roll(sc, 1, 0)))
        G[2, X] = jnp.where(clane == 0, f32(0.0), C[2, X] * ((0.25 * sc) * pltpu.roll(sc, 1, 1)))

    def coarse_step(x_ref, d_ref, to_x, to_d, X, number):
        keep, gain = coarse[number]
        x = x_ref[X]
        gy, gz = G[1, X], G[2, X]
        c = (A[X] - x) + G[0, X] * x_ref[X - 1] + G[0, X + 1] * x_ref[X + 1]
        c = c + gy * pltpu.roll(x, 1, 0) + pltpu.roll(gy * x, 23, 0)
        c = c + gz * pltpu.roll(x, 1, 1) + pltpu.roll(gz * x, 127, 1)
        step_dir = keep * d_ref[X] + gain * c
        return x + step_dir, step_dir

    for message in e_one:
        message.wait_recv()
    for X in range(10):
        start = coarse[0][1] * A[X]
        XA[X] = start
        CD[X] = start
    now, later = XA, XB
    for number in range(1, 4):
        for X in range(number, 10 - number):
            later[X], CD[X] = coarse_step(now, CD, None, None, X, number)
        now, later = later, now
    for X in range(CX0, CX0 + 2):
        new_x, new_d = coarse_step(now, CD, None, None, X, 4)
        B[0, X, pl.ds(CR0, CRN), :] = new_x[CR0:CR0 + CRN]
        B[1, X, pl.ds(CR0, CRN), :] = new_d[CR0:CR0 + CRN]
    e_two = coarse_messages(B, (pl.ds(0, 2),), b_send, b_recv)
    for message in e_two:
        message.wait_recv()
    now, now_d = B.at[0], B.at[1]
    for number, later in ((5, XA), (6, XB), (7, XA)):
        for X in range(number - 4, 14 - number):
            later[X], CD[X] = coarse_step(now, now_d, None, None, X, number)
        now, now_d = later, CD

    for message in late:
        message.wait_recv()
    spread_z = jnp.where(
        lax.shift_right_logical(lax.broadcasted_iota(jnp.int32, (128, 256), 1), 1) == lax.broadcasted_iota(jnp.int32, (128, 256), 0),
        f32(1.0), f32(0.0))
    spread_y = jnp.where(
        lax.shift_right_logical(lax.broadcasted_iota(jnp.int32, (40, 24), 0) + (2 * CR0 - FR0), 1) == lax.broadcasted_iota(jnp.int32, (40, 24), 1),
        f32(1.0), f32(0.0))
    corr = jnp.concatenate([C[3, X] * now[X] for X in range(3, 7)], 0)
    corr = dot(corr, spread_z)
    for X in range(4):
        fine_corr = dot(spread_y, corr[24 * X:24 * X + 24])
        fine_corr = jnp.stack([fine_corr[:, :128], fine_corr[:, 128:]])
        for x in (2 * X + 1, 2 * X + 2):
            W2[x] = (L2[x] + fine_corr) * (row_mask * slab_in(x))

    def third_body(x, carry):
        return first_step(W2, W1)(x, carry)

    lax.fori_loop(2, 8, third_body, 0)
    for x in range(FX0, FX1):
        last = second_step(x)
        for h in range(2):
            out[x - FX0, :, 128 * h:128 * h + 128] = last[h, FR0:FR0 + FRN]

    for message in first + coefs + e_one + late + e_two:
        message.wait_send()


def body(source, guess, mass_coef, diffusion):
    vmem = pltpu.VMEM
    fine_slabs = lambda: vmem((10, 2, 40, 128), jnp.float32)
    coarse_slabs = lambda: vmem((10, 24, 128), jnp.float32)
    n_rim, n_near, n_ring = len(rim_messages()), len(NEAR), len(RING)
    dma = pltpu.SemaphoreType.DMA
    return pl.pallas_call(
        kernel,
        out_shape=jax.ShapeDtypeStruct((4, 32, 256), jnp.float32),
        in_specs=[pl.BlockSpec(memory_space=pl.ANY)] * 4,
        out_specs=pl.BlockSpec(memory_space=pltpu.VMEM),
        scratch_shapes=[
            vmem((4, 10, 2, 40, 128), jnp.float32),
            fine_slabs(), fine_slabs(), fine_slabs(), fine_slabs(), fine_slabs(),
            fine_slabs(), fine_slabs(), fine_slabs(), fine_slabs(), fine_slabs(),
            vmem((4, 10, 24, 128), jnp.float32),
            vmem((3, 10, 24, 128), jnp.float32),
            coarse_slabs(),
            vmem((2, 10, 24, 128), jnp.float32),
            coarse_slabs(), coarse_slabs(), coarse_slabs(),
            dma((4, 2)),
            dma((n_rim,)), dma((n_rim,)),
            dma((n_near,)), dma((n_near,)),
            dma((n_near,)), dma((n_near,)),
            dma((n_near,)), dma((n_near,)),
            dma((n_ring,)), dma((n_ring,)),
        ],
        compiler_params=pltpu.CompilerParams(collective_id=0, has_side_effects=True, vmem_limit_bytes=48 * 2**20),
        name="cycle",
    )(source, guess, mass_coef, diffusion)


def solution(mesh):
    spec = P("box", "sub", None)
    return jax.shard_map(body, mesh=mesh, in_specs=(spec,) * 4, out_specs=spec, check_vma=False)
```

```python
import functools

import jax
import jax.numpy as jnp
from jax import lax
from jax.experimental import pallas as pl
from jax.experimental.pallas import tpu as pltpu
from jax.sharding import PartitionSpec as P

MESH = pl.DeviceIdType.MESH
CHEB_C = 8
FINE_LOW = 0.25
FINE_HIGH = 2.0
COARSE_LOW = 0.05
COARSE_HIGH = 2.0

FX0, FX1, FR0, FRN = 3, 7, 4, 32
CX0, CR0, CRN = 4, 4, 16
GUESS, DIFF, SOURCE, MASS = 0, 1, 2, 3

NEAR = [(i, j) for i in (-2, 2, -1, 1) for j in (-1, 1)] + [(-2, 0), (2, 0), (0, -1), (0, 1), (-1, 0), (1, 0)]
RING = [(i, j) for i in (-1, 1) for j in (-1, 1)] + [(0, -1), (0, 1), (-1, 0), (1, 0)]


def cheb_coeffs(count_steps, low_end, high_end):
    center_val = (high_end + low_end) / 2.0
    half_width = (high_end - low_end) / 2.0
    sigma_val = center_val / half_width
    factor_prev = 1.0 / sigma_val
    coeffs_list = [(0.0, 1.0 / center_val)]
    for number in range(1, count_steps):
        factor_next = 1.0 / (2.0 * sigma_val - factor_prev)
        coeffs_list.append((factor_next * factor_prev, 2.0 * factor_next / half_width))
        factor_prev = factor_next
    return coeffs_list


def coarse_rows(os):
    if os == 1:
        return pl.ds(CR0 + CRN - 4, 4), pl.ds(0, 4)
    if os == -1:
        return pl.ds(CR0, 4), pl.ds(CR0 + CRN, 4)
    return pl.ds(CR0, CRN), pl.ds(CR0, CRN)


def fine_cut(o, start, size, width):
    if o == 1:
        return pl.ds(start + size - width, width), pl.ds(start - width, width)
    if o == -1:
        return pl.ds(start, width), pl.ds(start + size, width)
    return pl.ds(start, size), pl.ds(start, size)


def rim_messages():
    own_x, own_rows, all_four = pl.ds(FX0, 4), pl.ds(FR0, FRN), pl.ds(0, 4)
    beside = []
    for j in (-1, 1):
        beside.append(((0, j), all_four, own_x, own_x) + fine_cut(j, FR0, FRN, 3))
    for i in (-1, 1):
        for j in (-1, 1):
            beside.append(((i, j), all_four) + fine_cut(i, FX0, 4, 2) + fine_cut(j, FR0, FRN, 2))
    ranks = []
    for depth in range(3):
        arrays = all_four if depth < 2 else pl.ds(0, 2)
        ranks.append([
            ((-1, 0), arrays, pl.ds(FX0 + depth, 1), pl.ds(FX1 + depth, 1), own_rows, own_rows),
            ((1, 0), arrays, pl.ds(FX1 - 1 - depth, 1), pl.ds(FX0 - 1 - depth, 1), own_rows, own_rows)])
    return [beside] + ranks


def dot(a, b):
    return jnp.dot(a, b, precision=lax.Precision.HIGHEST, preferred_element_type=jnp.float32)


def kernel(source, guess, mass, diff, out, F, FX, FY, FZ, DIAG, INV, W1, W2, DIR, RES, L2, C, G, A, B, XA, XB, CD,
           load_sem, r_send, r_recv, c_send, c_recv, e_send, e_recv, b_send, b_recv, l_send, l_recv):
    f32 = jnp.float32
    nbox, nsub = lax.axis_size("box"), lax.axis_size("sub")
    b, s = lax.axis_index("box"), lax.axis_index("sub")

    def both(p, q):
        return jnp.logical_and(p, q)

    def exists(o):
        box_in = {-2: b > 1, -1: b > 0, 0: None, 1: b < nbox - 1, 2: b < nbox - 2}[o[0]]
        sub_in = {-1: s > 0, 0: None, 1: s < nsub - 1}[o[1]]
        if box_in is None or sub_in is None:
            return sub_in if box_in is None else box_in
        return both(box_in, sub_in)

    inner = both(both(b > 1, b < nbox - 2), both(s > 0, s < nsub - 1))
    rim = jnp.logical_not(inner)

    def each(messages, act, back):
        @pl.when(inner)
        def _():
            for _, message in messages:
                act(message)

        @pl.when(rim)
        def _():
            for o, message in messages:
                pl.when(exists((-o[0], -o[1]) if back else o))(functools.partial(act, message))

    def start(messages):
        each(messages, lambda m: m.start(), False)

    def arrived(messages):
        each(messages, lambda m: m.wait_recv(), True)

    def left(messages):
        each(messages, lambda m: m.wait_send(), False)

    def message(o, src, dst, send, recv):
        return o, pltpu.make_async_remote_copy(
            src_ref=src, dst_ref=dst, send_sem=send, recv_sem=recv, device_id=(b + o[0], s + o[1]), device_id_type=MESH)

    loads = []
    for k, ref in enumerate((guess, diff, source, mass)):
        for h in range(2):
            loads.append(pltpu.make_async_copy(
                ref.at[:, :, pl.ds(128 * h, 128)], F.at[k, pl.ds(FX0, 4), h, pl.ds(FR0, FRN)], load_sem.at[k, h]))
            loads[-1].start()
    def outside(x_cut, row_cut, X_cut, coarse_row_cut, n_x, n_rows, n_X, n_coarse_rows):
        F[0:3, x_cut, :, row_cut] = jnp.zeros((3, n_x, 2, n_rows, 128), f32)
        F[3:4, x_cut, :, row_cut] = jnp.ones((1, n_x, 2, n_rows, 128), f32)
        L2[x_cut, :, row_cut] = jnp.zeros((n_x, 2, n_rows, 128), f32)
        C[:, X_cut, coarse_row_cut] = jnp.zeros((4, n_X, n_coarse_rows, 128), f32)
        A[X_cut, coarse_row_cut] = jnp.zeros((n_X, n_coarse_rows, 128), f32)
        B[:, X_cut, coarse_row_cut] = jnp.zeros((2, n_X, n_coarse_rows, 128), f32)

    def blank():
        every, lower, upper = slice(None), slice(0, 2), slice(8, 10)
        pl.when(b == 0)(lambda: outside(slice(0, FX0), every, slice(0, 4), every, FX0, 40, 4, 24))
        pl.when(b == nbox - 1)(lambda: outside(slice(FX1, 10), every, slice(6, 10), every, 10 - FX1, 40, 4, 24))
        pl.when(s == 0)(lambda: outside(every, slice(0, 4), every, slice(0, 4), 10, 4, 10, 4))
        pl.when(s == nsub - 1)(lambda: outside(every, slice(36, 40), every, slice(20, 24), 10, 4, 10, 4))

        @pl.when(b == 1)
        def _():
            C[:, lower] = jnp.zeros((4, 2, 24, 128), f32)
            A[lower] = jnp.zeros((2, 24, 128), f32)
            B[:, lower] = jnp.zeros((2, 2, 24, 128), f32)

        @pl.when(b == nbox - 2)
        def _():
            C[:, upper] = jnp.zeros((4, 2, 24, 128), f32)
            A[upper] = jnp.zeros((2, 24, 128), f32)
            B[:, upper] = jnp.zeros((2, 2, 24, 128), f32)

    barrier = pltpu.get_barrier_semaphore()

    def greet(o):
        pl.semaphore_signal(barrier, inc=1, device_id=(b + o[0], s + o[1]), device_id_type=MESH)

    for o in reversed(NEAR):
        pl.when(exists(o))(functools.partial(greet, o))
    pl.when(rim)(blank)
    for load in loads:
        load.wait()

    first, k = [], 0
    for group in rim_messages():
        first.append([])
        for o, arrays, xs, xd, rs, rd in group:
            first[-1].append(message(o, F.at[arrays, xs, :, rs], F.at[arrays, xd, :, rd], r_send.at[k], r_recv.at[k]))
            k += 1
    n_box = jnp.minimum(b, 2) + jnp.minimum(nbox - 1 - b, 2)
    n_sub = jnp.minimum(s, 1) + jnp.minimum(nsub - 1 - s, 1)
    pl.semaphore_wait(barrier, (n_box + 1) * (n_sub + 1) - 1)
    start([m for group in first for m in group])

    lane = lax.broadcasted_iota(jnp.int32, (256, 128), 0)
    cell = lax.broadcasted_iota(jnp.int32, (256, 128), 1)
    z_mean = jnp.where(lax.shift_right_logical(lane, 1) == cell, f32(0.5), f32(0.0))
    z_low = jnp.where(lax.shift_right_logical(lane + 1, 1) == cell, f32(0.5), f32(0.0))
    z_high = jnp.where(lax.shift_right_logical(lane + 1, 1) == cell + 1, f32(0.5), f32(0.0))
    row = lax.broadcasted_iota(jnp.int32, (2, 40, 128), 1)
    row_in = jnp.logical_and(jnp.logical_or(row >= FR0, s > 0), jnp.logical_or(row < FR0 + FRN, s < nsub - 1))
    row_mask = jnp.where(row_in, f32(1.0), f32(0.0))
    lane_f = lax.broadcasted_iota(jnp.int32, (2, 40, 128), 2)
    half = lax.broadcasted_iota(jnp.int32, (2, 40, 128), 0)
    z_first = jnp.logical_and(lane_f == 0, half == 0)
    z_last = jnp.logical_and(lane_f == 127, half == 1)

    def shift(v, edge, by):
        r = pltpu.roll(v, by, 2)
        return jnp.where(edge, jnp.stack([r[1], r[0]]), r)

    def from_below(v):
        return shift(v, lane_f == 0, 1)

    def from_above(v):
        return shift(v, lane_f == 127, 127)


    def slab_in(x):
        inside = jnp.logical_and(jnp.logical_or(x >= FX0, b > 0), jnp.logical_or(x < FX1, b < nbox - 1))
        return jnp.where(inside, f32(1.0), f32(0.0))

    def face(x):
        FX[x] = 0.5 * (F[DIFF, x - 1] + F[DIFF, x])

    def operator(x):
        d = F[DIFF, x]
        fy = 0.5 * (d + pltpu.roll(d, 1, 1))
        fz = 0.5 * (d + jnp.where(z_first, f32(0.0), from_below(d)))
        fz_high = 0.5 * (d + jnp.where(z_last, f32(0.0), from_above(d)))
        diag = F[MASS, x] + FX[x] + FX[x + 1] + fy + pltpu.roll(fy, 39, 1) + fz + fz_high
        FY[x] = fy
        FZ[x] = jnp.where(z_first, f32(0.0), fz)
        DIAG[x] = diag
        INV[x] = (row_mask * slab_in(x)) / diag

    def defect(u_ref, x):
        u = u_ref[x]
        fy, fz = FY[x], FZ[x]
        around = FX[x] * u_ref[x - 1] + FX[x + 1] * u_ref[x + 1]
        around = around + fy * pltpu.roll(u, 1, 1) + pltpu.roll(fy * u, 39, 1)
        around = around + fz * from_below(u) + from_above(fz * u)
        return (F[SOURCE, x] - DIAG[x] * u) + around, u

    fine = cheb_coeffs(2, FINE_LOW, FINE_HIGH)
    coarse = cheb_coeffs(CHEB_C, COARSE_LOW, COARSE_HIGH)

    def first_step(u_ref, to_ref, x):
        c, u = defect(u_ref, x)
        step_dir = (fine[0][1] * INV[x]) * c
        DIR[x] = step_dir
        to_ref[x] = u + step_dir

    def second_step(x):
        c, u = defect(W1, x)
        return u + (fine[1][0] * DIR[x] + (fine[1][1] * INV[x]) * c)

    def over(lo, hi, work, step=1):
        def turn(k, carry):
            work(lo + step * k)
            return carry

        lax.fori_loop(0, (hi - lo + step - 1) // step, turn, 0)

    def with_operator(x):
        operator(x)
        first_step(F.at[GUESS], W1, x)

    def smooth(x):
        W2[x] = second_step(x)

    def find_residual(x):
        RES[x] = defect(W2, x)[0]

    arrived(first[0])
    over(4, 7, face)
    with jax.named_scope("rank_one"):
        arrived(first[1])
    with jax.named_scope("work_one"):
        over(3, 8, face, 4)
        over(3, 7, with_operator)
    with jax.named_scope("coarse_coefficients"):
        def rows(ref, x, start):
            return ref[x, :, pl.ds(start, 16, 2), :]

        def wide(parts):
            return jnp.concatenate([jnp.concatenate([v[0], v[1]], 1) for v in parts], 0)


        D, M = F.at[DIFF], F.at[MASS]
        pair = {x: rows(D, x, FR0) + rows(D, x, FR0 + 1) for x in range(FX0 - 1, FX1 + 1)}
        low_y = {x: rows(D, x, FR0 - 1) + rows(D, x, FR0) for x in range(FX0, FX1)}
        high_y = {x: rows(D, x, FR0 + 1) + rows(D, x, FR0 + 2) for x in range(FX0, FX1)}
        in_mean, in_z = [], []
        for X in range(2):
            x = FX0 + 2 * X
            face_low, face_high = 0.25 * (pair[x - 1] + pair[x]), 0.25 * (pair[x + 1] + pair[x + 2])
            y_low, y_high = 0.25 * (low_y[x] + low_y[x + 1]), 0.25 * (high_y[x] + high_y[x + 1])
            mean_mass = 0.25 * (rows(M, x, FR0) + rows(M, x, FR0 + 1) + rows(M, x + 1, FR0) + rows(M, x + 1, FR0 + 1))
            in_mean += [face_low, y_low, mean_mass + 0.25 * (face_low + face_high + y_low + y_high)]
            in_z.append(0.25 * (pair[x] + pair[x + 1]))
        means = dot(wide(in_mean), z_mean)
        over_z = wide(in_z)
        lows_z, highs_z = dot(over_z, z_low), dot(over_z, z_high)
        own_s = []
        for X in range(2):
            fx, fy, d = (means[(3 * X + k) * 16:(3 * X + k + 1) * 16] for k in range(3))
            fz = lows_z[16 * X:16 * X + 16]
            d = d + 0.25 * (fz + highs_z[16 * X:16 * X + 16])
            sc = lax.rsqrt(d)
            sc = sc * (1.5 - 0.5 * d * sc * sc)
            own_s.append(sc)
            for k, v in enumerate((fx, fy, fz, sc)):
                C[k, CX0 + X, pl.ds(CR0, CRN), :] = v

    def coarse_messages(src, lead, sends, recvs):
        found = []
        for k, o in enumerate(NEAR):
            rs, rd = coarse_rows(o[1])
            found.append(message(
                o, src.at[lead + (pl.ds(CX0, 2), rs)], src.at[lead + (pl.ds(CX0 - 2 * o[0], 2), rd)], sends.at[k], recvs.at[k]))
        start(found)
        return found

    with jax.named_scope("rank_two"):
        arrived(first[2])
    with jax.named_scope("work_two"):
        over(2, 9, face, 6)
        over(2, 8, with_operator, 5)
        over(3, 7, smooth)
    coefs = coarse_messages(C, (pl.ds(0, 4),), c_send, c_recv)
    with jax.named_scope("rank_three"):
        arrived(first[3])
    with jax.named_scope("work_three"):
        over(1, 10, face, 8)
        over(1, 9, with_operator, 7)
        over(2, 8, smooth, 5)
        over(FX0, FX1, find_residual)

    means = []
    for X in range(2):
        x = FX0 + 2 * X
        means.append(0.25 * ((rows(RES, x, FR0) + rows(RES, x, FR0 + 1)) + (rows(RES, x + 1, FR0) + rows(RES, x + 1, FR0 + 1))))
    rhs = dot(wide(means), z_mean)
    for X in range(2):
        A[CX0 + X, pl.ds(CR0, CRN), :] = own_s[X] * rhs[16 * X:16 * X + 16]
    e_one = coarse_messages(A, (), e_send, e_recv)

    for x in range(FX0, FX1):
        L2[x, :, pl.ds(FR0, FRN), :] = W2[x, :, pl.ds(FR0, FRN), :]
    late = []
    for k, o in enumerate(RING):
        xs, xd = fine_cut(o[0], FX0, 4, 2)
        rs, rd = fine_cut(o[1], FR0, FRN, 2)
        late.append(message(o, L2.at[xs, :, rs], L2.at[xd, :, rd], l_send.at[k], l_recv.at[k]))
    start(late)

    with jax.named_scope("wait_coefficients"):
        arrived(coefs)
    clane = lax.broadcasted_iota(jnp.int32, (24, 128), 1)
    for X in range(10):
        sc = C[3, X]
        if X > 0:
            G[0, X] = C[0, X] * ((0.25 * sc) * C[3, X - 1])
        G[1, X] = C[1, X] * ((0.25 * sc) * pltpu.roll(sc, 1, 0))
        G[2, X] = jnp.where(clane == 0, f32(0.0), C[2, X] * ((0.25 * sc) * pltpu.roll(sc, 1, 1)))

    def coarse_step(x_ref, d_ref, to_x, to_d, X, number):
        keep, gain = coarse[number]
        x = x_ref[X]
        gy, gz = G[1, X], G[2, X]
        c = (A[X] - x) + G[0, X] * x_ref[X - 1] + G[0, X + 1] * x_ref[X + 1]
        c = c + gy * pltpu.roll(x, 1, 0) + pltpu.roll(gy * x, 23, 0)
        c = c + gz * pltpu.roll(x, 1, 1) + pltpu.roll(gz * x, 127, 1)
        step_dir = keep * d_ref[X] + gain * c
        return x + step_dir, step_dir

    with jax.named_scope("wait_right_hand_side"):
        left([m for group in first for m in group])
        arrived(e_one)
    for X in range(10):
        begin = coarse[0][1] * A[X]
        XA[X] = begin
        CD[X] = begin
    now, later = XA, XB
    for number in range(1, 4):
        for X in range(number, 10 - number):
            later[X], CD[X] = coarse_step(now, CD, None, None, X, number)
        now, later = later, now
    for X in range(CX0, CX0 + 2):
        new_x, new_d = coarse_step(now, CD, None, None, X, 4)
        B[0, X, pl.ds(CR0, CRN), :] = new_x[CR0:CR0 + CRN]
        B[1, X, pl.ds(CR0, CRN), :] = new_d[CR0:CR0 + CRN]
    e_two = coarse_messages(B, (pl.ds(0, 2),), b_send, b_recv)
    with jax.named_scope("wait_iterate"):
        left(coefs + e_one)
        arrived(late)
        left(late)
        arrived(e_two)
    now, now_d = B.at[0], B.at[1]
    for number, later in ((5, XA), (6, XB), (7, XA)):
        for X in range(number - 4, 14 - number):
            later[X], CD[X] = coarse_step(now, now_d, None, None, X, number)
        now, now_d = later, CD

    spread_z = jnp.where(
        lax.shift_right_logical(lax.broadcasted_iota(jnp.int32, (128, 256), 1), 1) == lax.broadcasted_iota(jnp.int32, (128, 256), 0),
        f32(1.0), f32(0.0))
    spread_y = jnp.where(
        lax.shift_right_logical(lax.broadcasted_iota(jnp.int32, (40, 24), 0) + (2 * CR0 - FR0), 1) == lax.broadcasted_iota(jnp.int32, (40, 24), 1),
        f32(1.0), f32(0.0))
    corr = jnp.concatenate([C[3, X] * now[X] for X in range(3, 7)], 0)
    corr = dot(corr, spread_z)
    for X in range(4):
        fine_corr = dot(spread_y, corr[24 * X:24 * X + 24])
        fine_corr = jnp.stack([fine_corr[:, :128], fine_corr[:, 128:]])
        for x in (2 * X + 1, 2 * X + 2):
            W2[x] = L2[x] + fine_corr

    over(2, 8, functools.partial(first_step, W2, W1))
    for x in range(FX0, FX1):
        last = second_step(x)
        for h in range(2):
            out[x - FX0, :, 128 * h:128 * h + 128] = last[h, FR0:FR0 + FRN]

    left(e_two)


def body(source, guess, mass_coef, diffusion):
    vmem = pltpu.VMEM
    fine_slabs = lambda: vmem((10, 2, 40, 128), jnp.float32)
    coarse_slabs = lambda: vmem((10, 24, 128), jnp.float32)
    n_rim, n_near, n_ring = sum(len(group) for group in rim_messages()), len(NEAR), len(RING)
    dma = pltpu.SemaphoreType.DMA
    return pl.pallas_call(
        kernel,
        out_shape=jax.ShapeDtypeStruct((4, 32, 256), jnp.float32),
        in_specs=[pl.BlockSpec(memory_space=pltpu.HBM)] * 4,
        out_specs=pl.BlockSpec(memory_space=pltpu.VMEM),
        scratch_shapes=[
            vmem((4, 10, 2, 40, 128), jnp.float32),
            fine_slabs(), fine_slabs(), fine_slabs(), fine_slabs(), fine_slabs(),
            fine_slabs(), fine_slabs(), fine_slabs(), fine_slabs(), fine_slabs(),
            vmem((4, 10, 24, 128), jnp.float32),
            vmem((3, 10, 24, 128), jnp.float32),
            coarse_slabs(),
            vmem((2, 10, 24, 128), jnp.float32),
            coarse_slabs(), coarse_slabs(), coarse_slabs(),
            dma((4, 2)),
            dma((n_rim,)), dma((n_rim,)),
            dma((n_near,)), dma((n_near,)),
            dma((n_near,)), dma((n_near,)),
            dma((n_near,)), dma((n_near,)),
            dma((n_ring,)), dma((n_ring,)),
        ],
        compiler_params=pltpu.CompilerParams(collective_id=0, has_side_effects=True, vmem_limit_bytes=63 * 2**20),
        name="cycle",
    )(source, guess, mass_coef, diffusion)


def solution(mesh):
    spec = P("box", "sub", None)
    return jax.shard_map(body, mesh=mesh, in_specs=(spec,) * 4, out_specs=spec, check_vma=False)
```

```python
import functools

import jax
import jax.numpy as jnp
from jax import lax
from jax.experimental import pallas as pl
from jax.experimental.pallas import tpu as pltpu
from jax.sharding import PartitionSpec as P

MESH = pl.DeviceIdType.MESH
CHEB_C = 8
FINE_LOW = 0.25
FINE_HIGH = 2.0
COARSE_LOW = 0.05
COARSE_HIGH = 2.0

FX0, FX1, FR0, FRN = 3, 7, 4, 32
CX0, CR0, CRN = 4, 4, 16
GUESS, DIFF, SOURCE, MASS = 0, 1, 2, 3

NEAR = [(i, j) for i in (-2, 2, -1, 1) for j in (-1, 1)] + [(-2, 0), (2, 0), (0, -1), (0, 1), (-1, 0), (1, 0)]
PLUS = [(0, 1), (1, -1), (1, 0), (1, 1), (2, -1), (2, 0), (2, 1)]
RING = [(i, j) for i in (-1, 1) for j in (-1, 1)] + [(0, -1), (0, 1), (-1, 0), (1, 0)]


def cheb_coeffs(count_steps, low_end, high_end):
    center_val = (high_end + low_end) / 2.0
    half_width = (high_end - low_end) / 2.0
    sigma_val = center_val / half_width
    factor_prev = 1.0 / sigma_val
    coeffs_list = [(0.0, 1.0 / center_val)]
    for number in range(1, count_steps):
        factor_next = 1.0 / (2.0 * sigma_val - factor_prev)
        coeffs_list.append((factor_next * factor_prev, 2.0 * factor_next / half_width))
        factor_prev = factor_next
    return coeffs_list


def coarse_rows(os):
    if os == 1:
        return pl.ds(CR0 + CRN - 4, 4), pl.ds(0, 4)
    if os == -1:
        return pl.ds(CR0, 4), pl.ds(CR0 + CRN, 4)
    return pl.ds(CR0, CRN), pl.ds(CR0, CRN)


def fine_cut(o, start, size, width):
    if o == 1:
        return pl.ds(start + size - width, width), pl.ds(start - width, width)
    if o == -1:
        return pl.ds(start, width), pl.ds(start + size, width)
    return pl.ds(start, size), pl.ds(start, size)


def rim_messages():
    own_x, own_rows, all_four = pl.ds(FX0, 4), pl.ds(FR0, FRN), pl.ds(0, 4)
    beside = []
    for j in (-1, 1):
        beside.append(((0, j), all_four, own_x, own_x) + fine_cut(j, FR0, FRN, 3))
    for i in (-1, 1):
        for j in (-1, 1):
            beside.append(((i, j), all_four) + fine_cut(i, FX0, 4, 2) + fine_cut(j, FR0, FRN, 2))
    ranks = []
    for depth in range(3):
        arrays = all_four if depth < 2 else pl.ds(0, 2)
        ranks.append([
            ((-1, 0), arrays, pl.ds(FX0 + depth, 1), pl.ds(FX1 + depth, 1), own_rows, own_rows),
            ((1, 0), arrays, pl.ds(FX1 - 1 - depth, 1), pl.ds(FX0 - 1 - depth, 1), own_rows, own_rows)])
    return [beside] + ranks


def dot(a, b):
    return jnp.dot(a, b, precision=lax.Precision.HIGHEST, preferred_element_type=jnp.float32)


def kernel(source, guess, mass, diff, out, F, FX, FY, FZ, DIAG, INV, W1, W2, DIR, RES, L2, C, G, A, B, XA, XB, CD,
           load_sem, r_send, r_recv, c_send, c_recv, e_send, e_recv, b_send, b_recv, l_send, l_recv, ready):
    f32 = jnp.float32
    nbox, nsub = lax.axis_size("box"), lax.axis_size("sub")
    b, s = lax.axis_index("box"), lax.axis_index("sub")

    def both(p, q):
        return jnp.logical_and(p, q)

    def exists(o):
        box_in = {-2: b > 1, -1: b > 0, 0: None, 1: b < nbox - 1, 2: b < nbox - 2}[o[0]]
        sub_in = {-1: s > 0, 0: None, 1: s < nsub - 1}[o[1]]
        if box_in is None or sub_in is None:
            return sub_in if box_in is None else box_in
        return both(box_in, sub_in)

    inner = both(both(b > 1, b < nbox - 2), both(s > 0, s < nsub - 1))
    rim = jnp.logical_not(inner)

    def each(messages, act, back):
        @pl.when(inner)
        def _():
            for _, message in messages:
                act(message)

        @pl.when(rim)
        def _():
            for o, message in messages:
                pl.when(exists((-o[0], -o[1]) if back else o))(functools.partial(act, message))

    def start(messages):
        each(messages, lambda m: m.start(), False)

    def arrived(messages):
        each(messages, lambda m: m.wait_recv(), True)

    def left(messages):
        each(messages, lambda m: m.wait_send(), False)

    def message(o, src, dst, send, recv):
        return o, pltpu.make_async_remote_copy(
            src_ref=src, dst_ref=dst, send_sem=send, recv_sem=recv, device_id=(b + o[0], s + o[1]), device_id_type=MESH)

    barrier = pltpu.get_barrier_semaphore()

    def greet(o, semaphore):
        pl.semaphore_signal(semaphore, inc=1, device_id=(b + o[0], s + o[1]), device_id_type=MESH)

    def minus(o):
        return (-o[0], -o[1])

    for o in PLUS:
        pl.when(exists(minus(o)))(functools.partial(greet, minus(o), barrier))
    loads = []
    for k, ref in enumerate((guess, diff, source, mass)):
        for h in range(2):
            loads.append(pltpu.make_async_copy(
                ref.at[:, :, pl.ds(128 * h, 128)], F.at[k, pl.ds(FX0, 4), h, pl.ds(FR0, FRN)], load_sem.at[k, h]))
            loads[-1].start()
    def outside(x_cut, row_cut, X_cut, coarse_row_cut, n_x, n_rows, n_X, n_coarse_rows):
        F[0:3, x_cut, :, row_cut] = jnp.zeros((3, n_x, 2, n_rows, 128), f32)
        F[3:4, x_cut, :, row_cut] = jnp.ones((1, n_x, 2, n_rows, 128), f32)
        L2[x_cut, :, row_cut] = jnp.zeros((n_x, 2, n_rows, 128), f32)
        C[:, X_cut, coarse_row_cut] = jnp.zeros((4, n_X, n_coarse_rows, 128), f32)
        A[X_cut, coarse_row_cut] = jnp.zeros((n_X, n_coarse_rows, 128), f32)
        B[:, X_cut, coarse_row_cut] = jnp.zeros((2, n_X, n_coarse_rows, 128), f32)

    def blank():
        every, lower, upper = slice(None), slice(0, 2), slice(8, 10)
        pl.when(b == 0)(lambda: outside(slice(0, FX0), every, slice(0, 4), every, FX0, 40, 4, 24))
        pl.when(b == nbox - 1)(lambda: outside(slice(FX1, 10), every, slice(6, 10), every, 10 - FX1, 40, 4, 24))
        pl.when(s == 0)(lambda: outside(every, slice(0, 4), every, slice(0, 4), 10, 4, 10, 4))
        pl.when(s == nsub - 1)(lambda: outside(every, slice(36, 40), every, slice(20, 24), 10, 4, 10, 4))

        @pl.when(b == 1)
        def _():
            C[:, lower] = jnp.zeros((4, 2, 24, 128), f32)
            A[lower] = jnp.zeros((2, 24, 128), f32)
            B[:, lower] = jnp.zeros((2, 2, 24, 128), f32)

        @pl.when(b == nbox - 2)
        def _():
            C[:, upper] = jnp.zeros((4, 2, 24, 128), f32)
            A[upper] = jnp.zeros((2, 24, 128), f32)
            B[:, upper] = jnp.zeros((2, 2, 24, 128), f32)

    for load in loads:
        load.wait()

    first, k = [], 0
    for group in rim_messages():
        first.append([])
        for o, arrays, xs, xd, rs, rd in group:
            first[-1].append(message(o, F.at[arrays, xs, :, rs], F.at[arrays, xd, :, rd], r_send.at[k], r_recv.at[k]))
            k += 1
    n_box = jnp.minimum(nbox - 1 - b, 2)
    n_sub = jnp.minimum(s, 1) + jnp.minimum(nsub - 1 - s, 1)
    n_plus = n_box * (n_sub + 1) + jnp.minimum(nsub - 1 - s, 1)
    pl.when(n_plus > 0)(lambda: pl.semaphore_wait(barrier, n_plus))
    for k, o in enumerate(PLUS):
        pl.when(exists(o))(functools.partial(greet, o, ready.at[k]))
    flat = [m for group in first for m in group]
    start([m for m in flat if m[0] in PLUS])

    def met(o):
        pl.when(exists(minus(o)))(lambda: pl.semaphore_wait(ready.at[PLUS.index(o)], 1))

    for o in ((1, -1), (0, 1), (1, 0), (1, 1)):
        met(o)
        start([m for m in flat if m[0] == minus(o)])
    pl.when(rim)(blank)

    lane = lax.broadcasted_iota(jnp.int32, (256, 128), 0)
    cell = lax.broadcasted_iota(jnp.int32, (256, 128), 1)
    z_mean = jnp.where(lax.shift_right_logical(lane, 1) == cell, f32(0.5), f32(0.0))
    z_low = jnp.where(lax.shift_right_logical(lane + 1, 1) == cell, f32(0.5), f32(0.0))
    z_high = jnp.where(lax.shift_right_logical(lane + 1, 1) == cell + 1, f32(0.5), f32(0.0))
    row = lax.broadcasted_iota(jnp.int32, (2, 40, 128), 1)
    row_in = jnp.logical_and(jnp.logical_or(row >= FR0, s > 0), jnp.logical_or(row < FR0 + FRN, s < nsub - 1))
    row_mask = jnp.where(row_in, f32(1.0), f32(0.0))
    lane_f = lax.broadcasted_iota(jnp.int32, (2, 40, 128), 2)
    half = lax.broadcasted_iota(jnp.int32, (2, 40, 128), 0)
    z_first = jnp.logical_and(lane_f == 0, half == 0)
    z_last = jnp.logical_and(lane_f == 127, half == 1)

    def shift(v, edge, by):
        r = pltpu.roll(v, by, 2)
        return jnp.where(edge, jnp.stack([r[1], r[0]]), r)

    def from_below(v):
        return shift(v, lane_f == 0, 1)

    def from_above(v):
        return shift(v, lane_f == 127, 127)


    def slab_in(x):
        inside = jnp.logical_and(jnp.logical_or(x >= FX0, b > 0), jnp.logical_or(x < FX1, b < nbox - 1))
        return jnp.where(inside, f32(1.0), f32(0.0))

    def face(x):
        FX[x] = 0.5 * (F[DIFF, x - 1] + F[DIFF, x])

    def operator(x):
        d = F[DIFF, x]
        fy = 0.5 * (d + pltpu.roll(d, 1, 1))
        fz = 0.5 * (d + jnp.where(z_first, f32(0.0), from_below(d)))
        fz_high = 0.5 * (d + jnp.where(z_last, f32(0.0), from_above(d)))
        diag = F[MASS, x] + FX[x] + FX[x + 1] + fy + pltpu.roll(fy, 39, 1) + fz + fz_high
        FY[x] = fy
        FZ[x] = jnp.where(z_first, f32(0.0), fz)
        DIAG[x] = diag
        INV[x] = (row_mask * slab_in(x)) / diag

    def defect(u_ref, x):
        u = u_ref[x]
        fy, fz = FY[x], FZ[x]
        around = FX[x] * u_ref[x - 1] + FX[x + 1] * u_ref[x + 1]
        around = around + fy * pltpu.roll(u, 1, 1) + pltpu.roll(fy * u, 39, 1)
        around = around + fz * from_below(u) + from_above(fz * u)
        return (F[SOURCE, x] - DIAG[x] * u) + around, u

    fine = cheb_coeffs(2, FINE_LOW, FINE_HIGH)
    coarse = cheb_coeffs(CHEB_C, COARSE_LOW, COARSE_HIGH)

    def first_step(u_ref, to_ref, x):
        c, u = defect(u_ref, x)
        step_dir = (fine[0][1] * INV[x]) * c
        DIR[x] = step_dir
        to_ref[x] = u + step_dir

    def second_step(x):
        c, u = defect(W1, x)
        return u + (fine[1][0] * DIR[x] + (fine[1][1] * INV[x]) * c)

    def over(lo, hi, work, step=1):
        def turn(k, carry):
            work(lo + step * k)
            return carry

        lax.fori_loop(0, (hi - lo + step - 1) // step, turn, 0, unroll=True)

    def with_operator(x):
        operator(x)
        first_step(F.at[GUESS], W1, x)

    def smooth(x):
        W2[x] = second_step(x)

    def find_residual(x):
        RES[x] = defect(W2, x)[0]

    arrived(first[0])
    over(4, 7, face)
    with jax.named_scope("rank_one"):
        arrived(first[1])
    with jax.named_scope("work_one"):
        over(3, 8, face, 4)
        over(3, 7, with_operator)
    with jax.named_scope("coarse_coefficients"):
        def rows(ref, x, start):
            return ref[x, :, pl.ds(start, 16, 2), :]

        def wide(parts):
            return jnp.concatenate([jnp.concatenate([v[0], v[1]], 1) for v in parts], 0)


        D, M = F.at[DIFF], F.at[MASS]
        pair = {x: rows(D, x, FR0) + rows(D, x, FR0 + 1) for x in range(FX0 - 1, FX1 + 1)}
        low_y = {x: rows(D, x, FR0 - 1) + rows(D, x, FR0) for x in range(FX0, FX1)}
        high_y = {x: rows(D, x, FR0 + 1) + rows(D, x, FR0 + 2) for x in range(FX0, FX1)}
        in_mean, in_z = [], []
        for X in range(2):
            x = FX0 + 2 * X
            face_low, face_high = 0.25 * (pair[x - 1] + pair[x]), 0.25 * (pair[x + 1] + pair[x + 2])
            y_low, y_high = 0.25 * (low_y[x] + low_y[x + 1]), 0.25 * (high_y[x] + high_y[x + 1])
            mean_mass = 0.25 * (rows(M, x, FR0) + rows(M, x, FR0 + 1) + rows(M, x + 1, FR0) + rows(M, x + 1, FR0 + 1))
            in_mean += [face_low, y_low, mean_mass + 0.25 * (face_low + face_high + y_low + y_high)]
            in_z.append(0.25 * (pair[x] + pair[x + 1]))
        means = dot(wide(in_mean), z_mean)
        over_z = wide(in_z)
        lows_z, highs_z = dot(over_z, z_low), dot(over_z, z_high)
        own_s = []
        for X in range(2):
            fx, fy, d = (means[(3 * X + k) * 16:(3 * X + k + 1) * 16] for k in range(3))
            fz = lows_z[16 * X:16 * X + 16]
            d = d + 0.25 * (fz + highs_z[16 * X:16 * X + 16])
            sc = lax.rsqrt(d)
            sc = sc * (1.5 - 0.5 * d * sc * sc)
            own_s.append(sc)
            for k, v in enumerate((fx, fy, fz, sc)):
                C[k, CX0 + X, pl.ds(CR0, CRN), :] = v

    def coarse_messages(src, lead, sends, recvs):
        found = []
        for k, o in enumerate(NEAR):
            rs, rd = coarse_rows(o[1])
            found.append(message(
                o, src.at[lead + (pl.ds(CX0, 2), rs)], src.at[lead + (pl.ds(CX0 - 2 * o[0], 2), rd)], sends.at[k], recvs.at[k]))
        start(found)
        return found

    with jax.named_scope("rank_two"):
        arrived(first[2])
    with jax.named_scope("work_two"):
        over(2, 9, face, 6)
        over(2, 8, with_operator, 5)
        over(3, 7, smooth)
    for o in PLUS[4:]:
        met(o)
    coefs = coarse_messages(C, (pl.ds(0, 4),), c_send, c_recv)
    with jax.named_scope("rank_three"):
        arrived(first[3])
    with jax.named_scope("work_three"):
        over(1, 10, face, 8)
        over(1, 9, with_operator, 7)
        over(2, 8, smooth, 5)
        over(FX0, FX1, find_residual)

    means = []
    for X in range(2):
        x = FX0 + 2 * X
        means.append(0.25 * ((rows(RES, x, FR0) + rows(RES, x, FR0 + 1)) + (rows(RES, x + 1, FR0) + rows(RES, x + 1, FR0 + 1))))
    rhs = dot(wide(means), z_mean)
    for X in range(2):
        A[CX0 + X, pl.ds(CR0, CRN), :] = own_s[X] * rhs[16 * X:16 * X + 16]
    e_one = coarse_messages(A, (), e_send, e_recv)

    for x in range(FX0, FX1):
        L2[x, :, pl.ds(FR0, FRN), :] = W2[x, :, pl.ds(FR0, FRN), :]
    late = []
    for k, o in enumerate(RING):
        xs, xd = fine_cut(o[0], FX0, 4, 2)
        rs, rd = fine_cut(o[1], FR0, FRN, 2)
        late.append(message(o, L2.at[xs, :, rs], L2.at[xd, :, rd], l_send.at[k], l_recv.at[k]))
    start(late)

    with jax.named_scope("wait_coefficients"):
        arrived(coefs)
    clane = lax.broadcasted_iota(jnp.int32, (24, 128), 1)
    for X in range(10):
        sc = C[3, X]
        if X > 0:
            G[0, X] = C[0, X] * ((0.25 * sc) * C[3, X - 1])
        G[1, X] = C[1, X] * ((0.25 * sc) * pltpu.roll(sc, 1, 0))
        G[2, X] = jnp.where(clane == 0, f32(0.0), C[2, X] * ((0.25 * sc) * pltpu.roll(sc, 1, 1)))

    def coarse_step(x_ref, d_ref, to_x, to_d, X, number):
        keep, gain = coarse[number]
        x = x_ref[X]
        gy, gz = G[1, X], G[2, X]
        c = (A[X] - x) + G[0, X] * x_ref[X - 1] + G[0, X + 1] * x_ref[X + 1]
        c = c + gy * pltpu.roll(x, 1, 0) + pltpu.roll(gy * x, 23, 0)
        c = c + gz * pltpu.roll(x, 1, 1) + pltpu.roll(gz * x, 127, 1)
        step_dir = keep * d_ref[X] + gain * c
        return x + step_dir, step_dir

    with jax.named_scope("wait_right_hand_side"):
        left(flat)
        arrived(e_one)
    for X in range(10):
        begin = coarse[0][1] * A[X]
        XA[X] = begin
        CD[X] = begin
    now, later = XA, XB
    for number in range(1, 4):
        for X in range(number, 10 - number):
            later[X], CD[X] = coarse_step(now, CD, None, None, X, number)
        now, later = later, now
    for X in range(CX0, CX0 + 2):
        new_x, new_d = coarse_step(now, CD, None, None, X, 4)
        B[0, X, pl.ds(CR0, CRN), :] = new_x[CR0:CR0 + CRN]
        B[1, X, pl.ds(CR0, CRN), :] = new_d[CR0:CR0 + CRN]
    e_two = coarse_messages(B, (pl.ds(0, 2),), b_send, b_recv)
    with jax.named_scope("wait_iterate"):
        left(coefs + e_one)
        arrived(late)
        left(late)
        arrived(e_two)
    now, now_d = B.at[0], B.at[1]
    for number, later in ((5, XA), (6, XB), (7, XA)):
        for X in range(number - 4, 14 - number):
            later[X], CD[X] = coarse_step(now, now_d, None, None, X, number)
        now, now_d = later, CD

    spread_z = jnp.where(
        lax.shift_right_logical(lax.broadcasted_iota(jnp.int32, (128, 256), 1), 1) == lax.broadcasted_iota(jnp.int32, (128, 256), 0),
        f32(1.0), f32(0.0))
    spread_y = jnp.where(
        lax.shift_right_logical(lax.broadcasted_iota(jnp.int32, (40, 24), 0) + (2 * CR0 - FR0), 1) == lax.broadcasted_iota(jnp.int32, (40, 24), 1),
        f32(1.0), f32(0.0))
    corr = jnp.concatenate([C[3, X] * now[X] for X in range(3, 7)], 0)
    corr = dot(corr, spread_z)
    for X in range(4):
        fine_corr = dot(spread_y, corr[24 * X:24 * X + 24])
        fine_corr = jnp.stack([fine_corr[:, :128], fine_corr[:, 128:]])
        for x in (2 * X + 1, 2 * X + 2):
            W2[x] = L2[x] + fine_corr

    over(2, 8, functools.partial(first_step, W2, W1))
    for x in range(FX0, FX1):
        last = second_step(x)
        for h in range(2):
            out[x - FX0, :, 128 * h:128 * h + 128] = last[h, FR0:FR0 + FRN]

    left(e_two)


def body(source, guess, mass_coef, diffusion):
    vmem = pltpu.VMEM
    fine_slabs = lambda: vmem((10, 2, 40, 128), jnp.float32)
    coarse_slabs = lambda: vmem((10, 24, 128), jnp.float32)
    n_rim, n_near, n_ring = sum(len(group) for group in rim_messages()), len(NEAR), len(RING)
    dma = pltpu.SemaphoreType.DMA
    return pl.pallas_call(
        kernel,
        out_shape=jax.ShapeDtypeStruct((4, 32, 256), jnp.float32),
        in_specs=[pl.BlockSpec(memory_space=pltpu.HBM)] * 4,
        out_specs=pl.BlockSpec(memory_space=pltpu.VMEM),
        scratch_shapes=[
            vmem((4, 10, 2, 40, 128), jnp.float32),
            fine_slabs(), fine_slabs(), fine_slabs(), fine_slabs(), fine_slabs(),
            fine_slabs(), fine_slabs(), fine_slabs(), fine_slabs(), fine_slabs(),
            vmem((4, 10, 24, 128), jnp.float32),
            vmem((3, 10, 24, 128), jnp.float32),
            coarse_slabs(),
            vmem((2, 10, 24, 128), jnp.float32),
            coarse_slabs(), coarse_slabs(), coarse_slabs(),
            dma((4, 2)),
            dma((n_rim,)), dma((n_rim,)),
            dma((n_near,)), dma((n_near,)),
            dma((n_near,)), dma((n_near,)),
            dma((n_near,)), dma((n_near,)),
            dma((n_ring,)), dma((n_ring,)),
            pltpu.SemaphoreType.REGULAR((len(PLUS),)),
        ],
        compiler_params=pltpu.CompilerParams(collective_id=0, has_side_effects=True, vmem_limit_bytes=48 * 2**20),
        name="cycle",
    )(*[pltpu.with_memory_space_constraint(v, pltpu.HBM) for v in (source, guess, mass_coef, diffusion)])


def solution(mesh):
    spec = P("box", "sub", None)
    return jax.shard_map(body, mesh=mesh, in_specs=(spec,) * 4, out_specs=spec, check_vma=False)
```

```python
import functools

import jax
import jax.numpy as jnp
from jax import lax
from jax.experimental import pallas as pl
from jax.experimental.pallas import tpu as pltpu
from jax.sharding import PartitionSpec as P

MESH = pl.DeviceIdType.MESH
CHEB_C = 8
FINE_LOW = 0.25
FINE_HIGH = 2.0
COARSE_LOW = 0.05
COARSE_HIGH = 2.0

FX0, FX1, FR0, FRN = 3, 7, 4, 32
CX0, CR0, CRN = 4, 4, 16
GUESS, DIFF, SOURCE, MASS = 0, 1, 2, 3

NEAR = [(i, j) for i in (-2, 2, -1, 1) for j in (-1, 1)] + [(-2, 0), (2, 0), (0, -1), (0, 1), (-1, 0), (1, 0)]
PLUS = [(0, 1), (1, -1), (1, 0), (1, 1), (2, -1), (2, 0), (2, 1)]
LOW_Y, LOW_Z, LOW_X, ROOT = (0, 6), (1, 7), (2, 5), (3, 4)
C_SLOTS, A_SLOTS, B_SLOTS = 8, 2, 4
STEP, ITERATE = (0, 3), (1, 2)
RING = [(i, j) for i in (-1, 1) for j in (-1, 1)] + [(0, -1), (0, 1), (-1, 0), (1, 0)]


def cheb_coeffs(count_steps, low_end, high_end):
    center_val = (high_end + low_end) / 2.0
    half_width = (high_end - low_end) / 2.0
    sigma_val = center_val / half_width
    factor_prev = 1.0 / sigma_val
    coeffs_list = [(0.0, 1.0 / center_val)]
    for number in range(1, count_steps):
        factor_next = 1.0 / (2.0 * sigma_val - factor_prev)
        coeffs_list.append((factor_next * factor_prev, 2.0 * factor_next / half_width))
        factor_prev = factor_next
    return coeffs_list


def coarse_rows(os, width):
    if os == 1:
        return pl.ds(CR0 + CRN - width, width), pl.ds(CR0 - width, width)
    if os == -1:
        return pl.ds(CR0, width), pl.ds(CR0 + CRN, width)
    return pl.ds(CR0, CRN), pl.ds(CR0, CRN)


def coef_cut(o):
    return {2: (3, 5), -2: (0, 6)}.get(o[0], (0, C_SLOTS)) + (2 if abs(o[0]) == 2 else 4,)


def rhs_cut(o):
    if abs(o[0]) == 2 and o[1] != 0:
        return (1 if o[0] == 2 else 0), 1, 1
    return 0, A_SLOTS, (4 if o[0] == 0 else 3)


def iterate_cut(o):
    return {2: (1, 3), -2: (0, 3)}.get(o[0], (0, B_SLOTS)) + (2 if abs(o[0]) == 2 else 4,)


def fine_cut(o, start, size, width):
    if o == 1:
        return pl.ds(start + size - width, width), pl.ds(start - width, width)
    if o == -1:
        return pl.ds(start, width), pl.ds(start + size, width)
    return pl.ds(start, size), pl.ds(start, size)


def rim_messages():
    own_x, own_rows, all_four = pl.ds(FX0, 4), pl.ds(FR0, FRN), pl.ds(0, 4)
    beside = []
    for j in (-1, 1):
        beside.append(((0, j), all_four, own_x, own_x) + fine_cut(j, FR0, FRN, 3))
    for i in (-1, 1):
        for j in (-1, 1):
            beside.append(((i, j), all_four) + fine_cut(i, FX0, 4, 2) + fine_cut(j, FR0, FRN, 2))
    ranks = []
    for depth in range(3):
        arrays = all_four if depth < 2 else pl.ds(0, 2)
        ranks.append([
            ((-1, 0), arrays, pl.ds(FX0 + depth, 1), pl.ds(FX1 + depth, 1), own_rows, own_rows),
            ((1, 0), arrays, pl.ds(FX1 - 1 - depth, 1), pl.ds(FX0 - 1 - depth, 1), own_rows, own_rows)])
    return [beside] + ranks


def dot(a, b):
    return jnp.dot(a, b, precision=lax.Precision.HIGHEST, preferred_element_type=jnp.float32)


def kernel(source, guess, mass, diff, out, F, FX, FY, FZ, DIAG, INV, W1, W2, DIR, RES, L2, C, G, A, B, XA, XB, CD,
           load_sem, r_send, r_recv, c_send, c_recv, e_send, e_recv, b_send, b_recv, l_send, l_recv, ready):
    f32 = jnp.float32
    nbox, nsub = lax.axis_size("box"), lax.axis_size("sub")
    b, s = lax.axis_index("box"), lax.axis_index("sub")

    def both(p, q):
        return jnp.logical_and(p, q)

    def exists(o):
        box_in = {-2: b > 1, -1: b > 0, 0: None, 1: b < nbox - 1, 2: b < nbox - 2}[o[0]]
        sub_in = {-1: s > 0, 0: None, 1: s < nsub - 1}[o[1]]
        if box_in is None or sub_in is None:
            return sub_in if box_in is None else box_in
        return both(box_in, sub_in)

    inner = both(both(b > 1, b < nbox - 2), both(s > 0, s < nsub - 1))
    rim = jnp.logical_not(inner)

    def each(messages, act, back):
        @pl.when(inner)
        def _():
            for _, message in messages:
                act(message)

        @pl.when(rim)
        def _():
            for o, message in messages:
                pl.when(exists((-o[0], -o[1]) if back else o))(functools.partial(act, message))

    def start(messages):
        each(messages, lambda m: m.start(), False)

    def arrived(messages):
        each(messages, lambda m: m.wait_recv(), True)

    def left(messages):
        each(messages, lambda m: m.wait_send(), False)

    def message(o, src, dst, send, recv):
        return o, pltpu.make_async_remote_copy(
            src_ref=src, dst_ref=dst, send_sem=send, recv_sem=recv, device_id=(b + o[0], s + o[1]), device_id_type=MESH)

    barrier = pltpu.get_barrier_semaphore()

    def greet(o, semaphore):
        pl.semaphore_signal(semaphore, inc=1, device_id=(b + o[0], s + o[1]), device_id_type=MESH)

    def minus(o):
        return (-o[0], -o[1])

    origin = both(b == 0, s == 0)
    other = jnp.logical_not(origin)

    def is_origin(o):
        return both(b + o[0] == 0, s + o[1] == 0)

    def there(o):
        return both(exists(o), jnp.logical_not(is_origin(o)))

    MINUS = [minus(o) for o in PLUS]
    for o in PLUS:
        pl.when(both(exists(o), other))(functools.partial(greet, o, barrier))
    for o in MINUS:
        pl.when(is_origin(o))(functools.partial(greet, o, barrier))
    loads = []
    for k, ref in enumerate((guess, diff, source, mass)):
        for h in range(2):
            loads.append(pltpu.make_async_copy(
                ref.at[:, :, pl.ds(128 * h, 128)], F.at[k, pl.ds(FX0, 4), h, pl.ds(FR0, FRN)], load_sem.at[k, h]))
            loads[-1].start()
    def outside(x_cut, row_cut, X_cut, coarse_row_cut, n_x, n_rows, n_X, n_coarse_rows):
        F[0:3, x_cut, :, row_cut] = jnp.zeros((3, n_x, 2, n_rows, 128), f32)
        F[3:4, x_cut, :, row_cut] = jnp.ones((1, n_x, 2, n_rows, 128), f32)
        L2[x_cut, :, row_cut] = jnp.zeros((n_x, 2, n_rows, 128), f32)
        blank_coarse(X_cut, coarse_row_cut, n_X, n_coarse_rows)

    def blank_coarse(group_cut, row_cut, n_groups, n_rows):
        for ref, slots in ((C, C_SLOTS), (A, A_SLOTS), (B, B_SLOTS)):
            ref[group_cut, :, row_cut] = jnp.zeros((n_groups, slots, n_rows, 128), f32)

    def blank():
        every = slice(None)
        pl.when(b == 0)(lambda: outside(slice(0, FX0), every, slice(0, 2), every, FX0, 40, 2, 24))
        pl.when(b == nbox - 1)(lambda: outside(slice(FX1, 10), every, slice(3, 5), every, 10 - FX1, 40, 2, 24))
        pl.when(s == 0)(lambda: outside(every, slice(0, 4), every, slice(0, 4), 10, 4, 5, 4))
        pl.when(s == nsub - 1)(lambda: outside(every, slice(36, 40), every, slice(20, 24), 10, 4, 5, 4))
        pl.when(b == 1)(lambda: blank_coarse(slice(0, 1), every, 1, 24))
        pl.when(b == nbox - 2)(lambda: blank_coarse(slice(4, 5), every, 1, 24))

    for load in loads:
        load.wait()

    first, k = [], 0
    for group in rim_messages():
        first.append([])
        for o, arrays, xs, xd, rs, rd in group:
            first[-1].append(message(o, F.at[arrays, xs, :, rs], F.at[arrays, xd, :, rd], r_send.at[k], r_recv.at[k]))
            k += 1
    flat = [m for group in first for m in group]
    n_sub = jnp.minimum(s, 1) + jnp.minimum(nsub - 1 - s, 1)
    n_minus = jnp.minimum(b, 2) * (n_sub + 1) + jnp.minimum(s, 1)
    n_plus = jnp.minimum(nbox - 1 - b, 2) * (n_sub + 1) + jnp.minimum(nsub - 1 - s, 1)
    by_origin = both(both(b < 3, s < 2), other)

    def wait_barrier(count):
        pl.when(count > 0)(lambda: pl.semaphore_wait(barrier, count))

    pl.when(origin)(lambda: wait_barrier(n_plus))
    pl.when(by_origin)(lambda: wait_barrier(n_minus - 1))
    pl.when(jnp.logical_not(jnp.logical_or(origin, by_origin)))(lambda: wait_barrier(n_minus))

    def slot(o):
        return ready.at[NEAR.index(o)]

    for o in MINUS:
        pl.when(there(o))(functools.partial(greet, o, slot(minus(o))))
    for o in PLUS:
        pl.when(both(exists(o), origin))(functools.partial(greet, o, slot(minus(o))))

    def send(o):
        for m in flat:
            if m[0] == o:
                m[1].start()

    def send_met(o):
        pl.semaphore_wait(slot(o), 1)
        send(o)

    for o in MINUS[:4]:
        pl.when(there(o))(functools.partial(send, o))
    for o in PLUS[:4]:
        pl.when(both(exists(o), origin))(functools.partial(send, o))
    for o in PLUS[:4]:
        pl.when(both(exists(o), other))(functools.partial(send_met, o))
    for o in MINUS[:4]:
        pl.when(is_origin(o))(functools.partial(send_met, o))
    pl.when(rim)(blank)

    lane = lax.broadcasted_iota(jnp.int32, (256, 128), 0)
    cell = lax.broadcasted_iota(jnp.int32, (256, 128), 1)
    z_mean = jnp.where(lax.shift_right_logical(lane, 1) == cell, f32(0.5), f32(0.0))
    z_low = jnp.where(lax.shift_right_logical(lane + 1, 1) == cell, f32(0.5), f32(0.0))
    z_high = jnp.where(lax.shift_right_logical(lane + 1, 1) == cell + 1, f32(0.5), f32(0.0))
    row = lax.broadcasted_iota(jnp.int32, (2, 40, 128), 1)
    row_in = jnp.logical_and(jnp.logical_or(row >= FR0, s > 0), jnp.logical_or(row < FR0 + FRN, s < nsub - 1))
    row_mask = jnp.where(row_in, f32(1.0), f32(0.0))
    lane_f = lax.broadcasted_iota(jnp.int32, (2, 40, 128), 2)
    half = lax.broadcasted_iota(jnp.int32, (2, 40, 128), 0)
    z_first = jnp.logical_and(lane_f == 0, half == 0)
    z_last = jnp.logical_and(lane_f == 127, half == 1)

    def shift(v, edge, by):
        r = pltpu.roll(v, by, 2)
        return jnp.where(edge, jnp.stack([r[1], r[0]]), r)

    def from_below(v):
        return shift(v, lane_f == 0, 1)

    def from_above(v):
        return shift(v, lane_f == 127, 127)


    def slab_in(x):
        inside = jnp.logical_and(jnp.logical_or(x >= FX0, b > 0), jnp.logical_or(x < FX1, b < nbox - 1))
        return jnp.where(inside, f32(1.0), f32(0.0))

    def face(x):
        FX[x] = 0.5 * (F[DIFF, x - 1] + F[DIFF, x])

    def operator(x):
        d = F[DIFF, x]
        fy = 0.5 * (d + pltpu.roll(d, 1, 1))
        fz = 0.5 * (d + jnp.where(z_first, f32(0.0), from_below(d)))
        fz_high = 0.5 * (d + jnp.where(z_last, f32(0.0), from_above(d)))
        diag = F[MASS, x] + FX[x] + FX[x + 1] + fy + pltpu.roll(fy, 39, 1) + fz + fz_high
        FY[x] = fy
        FZ[x] = jnp.where(z_first, f32(0.0), fz)
        DIAG[x] = diag
        INV[x] = (row_mask * slab_in(x)) / diag

    def defect(u_ref, x):
        u = u_ref[x]
        fy, fz = FY[x], FZ[x]
        around = FX[x] * u_ref[x - 1] + FX[x + 1] * u_ref[x + 1]
        around = around + fy * pltpu.roll(u, 1, 1) + pltpu.roll(fy * u, 39, 1)
        around = around + fz * from_below(u) + from_above(fz * u)
        return (F[SOURCE, x] - DIAG[x] * u) + around, u

    fine = cheb_coeffs(2, FINE_LOW, FINE_HIGH)
    coarse = cheb_coeffs(CHEB_C, COARSE_LOW, COARSE_HIGH)

    def first_step(u_ref, to_ref, x):
        c, u = defect(u_ref, x)
        step_dir = (fine[0][1] * INV[x]) * c
        DIR[x] = step_dir
        to_ref[x] = u + step_dir

    def second_step(x):
        c, u = defect(W1, x)
        return u + (fine[1][0] * DIR[x] + (fine[1][1] * INV[x]) * c)

    def over(lo, hi, work, step=1):
        def turn(k, carry):
            work(lo + step * k)
            return carry

        lax.fori_loop(0, (hi - lo + step - 1) // step, turn, 0, unroll=True)

    def with_operator(x):
        operator(x)
        first_step(F.at[GUESS], W1, x)

    def smooth(x):
        W2[x] = second_step(x)

    def find_residual(x):
        RES[x] = defect(W2, x)[0]

    arrived(first[0])
    over(4, 7, face)
    with jax.named_scope("rank_one"):
        arrived(first[1])
    with jax.named_scope("coarse_coefficients"):
        def rows(ref, x, start):
            return ref[x, :, pl.ds(start, 16, 2), :]

        def wide(parts):
            return jnp.concatenate([jnp.concatenate([v[0], v[1]], 1) for v in parts], 0)


        D, M = F.at[DIFF], F.at[MASS]
        pair = {x: rows(D, x, FR0) + rows(D, x, FR0 + 1) for x in range(FX0 - 1, FX1 + 1)}
        low_y = {x: rows(D, x, FR0 - 1) + rows(D, x, FR0) for x in range(FX0, FX1)}
        high_y = {x: rows(D, x, FR0 + 1) + rows(D, x, FR0 + 2) for x in range(FX0, FX1)}
        in_mean, in_z = [], []
        for X in range(2):
            x = FX0 + 2 * X
            face_low, face_high = 0.25 * (pair[x - 1] + pair[x]), 0.25 * (pair[x + 1] + pair[x + 2])
            y_low, y_high = 0.25 * (low_y[x] + low_y[x + 1]), 0.25 * (high_y[x] + high_y[x + 1])
            mean_mass = 0.25 * (rows(M, x, FR0) + rows(M, x, FR0 + 1) + rows(M, x + 1, FR0) + rows(M, x + 1, FR0 + 1))
            in_mean += [face_low, y_low, mean_mass + 0.25 * (face_low + face_high + y_low + y_high)]
            in_z.append(0.25 * (pair[x] + pair[x + 1]))
        means = dot(wide(in_mean), z_mean)
        over_z = wide(in_z)
        lows_z, highs_z = dot(over_z, z_low), dot(over_z, z_high)
        own_s = []
        for X in range(2):
            fx, fy, d = (means[(3 * X + k) * 16:(3 * X + k + 1) * 16] for k in range(3))
            fz = lows_z[16 * X:16 * X + 16]
            d = d + 0.25 * (fz + highs_z[16 * X:16 * X + 16])
            sc = lax.rsqrt(d)
            sc = sc * (1.5 - 0.5 * d * sc * sc)
            own_s.append(sc)
            for kind, v in ((LOW_X, fx), (LOW_Y, fy), (LOW_Z, fz), (ROOT, sc)):
                C[2, kind[X], pl.ds(CR0, CRN), :] = v

    def coarse_messages(src, cut, sends, recvs):
        found = []
        for k, o in enumerate(NEAR):
            at, count, width = cut(o)
            rs, rd = coarse_rows(o[1], width)
            found.append(message(
                o, src.at[2, pl.ds(at, count), rs], src.at[2 - o[0], pl.ds(at, count), rd], sends.at[k], recvs.at[k]))
        start(found)
        return found

    def meet(o):
        pl.semaphore_wait(slot(o), 1)

    for o in PLUS[4:]:
        pl.when(both(exists(o), other))(functools.partial(meet, o))
    for o in MINUS[4:]:
        pl.when(is_origin(o))(functools.partial(meet, o))
    coefs = coarse_messages(C, coef_cut, c_send, c_recv)

    with jax.named_scope("work_one"):
        over(3, 8, face, 4)
        over(3, 7, with_operator)
    with jax.named_scope("rank_two"):
        arrived(first[2])
    with jax.named_scope("work_two"):
        over(2, 9, face, 6)
        over(2, 8, with_operator, 5)
        over(3, 7, smooth)
    with jax.named_scope("rank_three"):
        arrived(first[3])
    with jax.named_scope("work_three"):
        over(1, 10, face, 8)
        over(1, 9, with_operator, 7)
        over(2, 8, smooth, 5)
        over(FX0, FX1, find_residual)

    means = []
    for X in range(2):
        x = FX0 + 2 * X
        means.append(0.25 * ((rows(RES, x, FR0) + rows(RES, x, FR0 + 1)) + (rows(RES, x + 1, FR0) + rows(RES, x + 1, FR0 + 1))))
    rhs = dot(wide(means), z_mean)
    for X in range(2):
        A[2, X, pl.ds(CR0, CRN), :] = own_s[X] * rhs[16 * X:16 * X + 16]
    e_one = coarse_messages(A, rhs_cut, e_send, e_recv)

    for x in range(FX0 - 1, FX1 + 1):
        L2[x, :, pl.ds(FR0, FRN), :] = W2[x, :, pl.ds(FR0, FRN), :]
    late = []
    for k, o in enumerate(RING):
        if o[1] == 0:
            at_x = FX1 - 2 if o[0] == 1 else FX0 + 1
            xs, xd = pl.ds(at_x, 1), pl.ds(at_x - 4 * o[0], 1)
        else:
            xs, xd = fine_cut(o[0], FX0, 4, 1)
        rs, rd = fine_cut(o[1], FR0, FRN, 2 if o[0] == 0 else 1)
        late.append(message(o, L2.at[xs, :, rs], L2.at[xd, :, rd], l_send.at[k], l_recv.at[k]))
    start(late)

    with jax.named_scope("wait_coefficients"):
        arrived(coefs)
    clane = lax.broadcasted_iota(jnp.int32, (24, 128), 1)

    def coef(kind, X):
        return C[X // 2, kind[X % 2]]

    for X in range(1, 10):
        sc = coef(ROOT, X)
        G[0, X] = coef(LOW_X, X) * ((0.25 * sc) * coef(ROOT, X - 1))
        if X < 9:
            G[1, X] = coef(LOW_Y, X) * ((0.25 * sc) * pltpu.roll(sc, 1, 0))
            G[2, X] = jnp.where(clane == 0, f32(0.0), coef(LOW_Z, X) * ((0.25 * sc) * pltpu.roll(sc, 1, 1)))

    def coarse_step(iterate, step_of, X, number):
        keep, gain = coarse[number]
        x = iterate(X)
        gy, gz = G[1, X], G[2, X]
        c = (A[X // 2, X % 2] - x) + G[0, X] * iterate(X - 1) + G[0, X + 1] * iterate(X + 1)
        c = c + gy * pltpu.roll(x, 1, 0) + pltpu.roll(gy * x, 23, 0)
        c = c + gz * pltpu.roll(x, 1, 1) + pltpu.roll(gz * x, 127, 1)
        step_dir = keep * step_of(X) + gain * c
        return x + step_dir, step_dir

    with jax.named_scope("wait_right_hand_side"):
        left(flat)
        arrived(e_one)
    for X in range(10):
        begin = coarse[0][1] * A[X // 2, X % 2]
        XA[X] = begin
        CD[X] = begin

    def of(ref):
        return lambda X: ref[X]

    now, later = XA, XB
    for number in range(1, 4):
        for X in range(number, 10 - number):
            later[X], CD[X] = coarse_step(of(now), of(CD), X, number)
        now, later = later, now
    for X in range(CX0, CX0 + 2):
        new_x, new_d = coarse_step(of(now), of(CD), X, 4)
        B[2, ITERATE[X % 2], pl.ds(CR0, CRN), :] = new_x[CR0:CR0 + CRN]
        B[2, STEP[X % 2], pl.ds(CR0, CRN), :] = new_d[CR0:CR0 + CRN]
    e_two = coarse_messages(B, iterate_cut, b_send, b_recv)
    with jax.named_scope("wait_iterate"):
        left(coefs + e_one)
        arrived(late)
        left(late)
        arrived(e_two)
    iterate, step_of = (lambda X: B[X // 2, ITERATE[X % 2]]), (lambda X: B[X // 2, STEP[X % 2]])
    for number, later in ((5, XA), (6, XB), (7, XA)):
        for X in range(number - 4, 14 - number):
            later[X], CD[X] = coarse_step(iterate, step_of, X, number)
        iterate, step_of = of(later), of(CD)

    spread_z = jnp.where(
        lax.shift_right_logical(lax.broadcasted_iota(jnp.int32, (128, 256), 1), 1) == lax.broadcasted_iota(jnp.int32, (128, 256), 0),
        f32(1.0), f32(0.0))
    spread_y = jnp.where(
        lax.shift_right_logical(lax.broadcasted_iota(jnp.int32, (40, 24), 0) + (2 * CR0 - FR0), 1) == lax.broadcasted_iota(jnp.int32, (40, 24), 1),
        f32(1.0), f32(0.0))
    crow = lax.broadcasted_iota(jnp.int32, (24, 128), 0)
    in_rim = both(crow >= CR0 - 1, crow <= CR0 + CRN)
    corr = jnp.concatenate([jnp.where(in_rim, coef(ROOT, X) * iterate(X), f32(0.0)) for X in range(3, 7)], 0)
    corr = dot(corr, spread_z)
    for X in range(4):
        fine_corr = dot(spread_y, corr[24 * X:24 * X + 24])
        fine_corr = jnp.stack([fine_corr[:, :128], fine_corr[:, 128:]])
        for x in (2 * X + 1, 2 * X + 2):
            W2[x] = L2[x] + fine_corr

    over(2, 8, functools.partial(first_step, W2, W1))
    for x in range(FX0, FX1):
        last = second_step(x)
        for h in range(2):
            out[x - FX0, :, 128 * h:128 * h + 128] = last[h, FR0:FR0 + FRN]

    left(e_two)


def body(source, guess, mass_coef, diffusion):
    vmem = pltpu.VMEM
    fine_slabs = lambda: vmem((10, 2, 40, 128), jnp.float32)
    coarse_slabs = lambda: vmem((10, 24, 128), jnp.float32)
    n_rim, n_near, n_ring = sum(len(group) for group in rim_messages()), len(NEAR), len(RING)
    dma = pltpu.SemaphoreType.DMA
    return pl.pallas_call(
        kernel,
        out_shape=jax.ShapeDtypeStruct((4, 32, 256), jnp.float32),
        in_specs=[pl.BlockSpec(memory_space=pltpu.HBM)] * 4,
        out_specs=pl.BlockSpec(memory_space=pltpu.VMEM),
        scratch_shapes=[
            vmem((4, 10, 2, 40, 128), jnp.float32),
            fine_slabs(), fine_slabs(), fine_slabs(), fine_slabs(), fine_slabs(),
            fine_slabs(), fine_slabs(), fine_slabs(), fine_slabs(), fine_slabs(),
            vmem((5, C_SLOTS, 24, 128), jnp.float32),
            vmem((3, 10, 24, 128), jnp.float32),
            vmem((5, A_SLOTS, 24, 128), jnp.float32),
            vmem((5, B_SLOTS, 24, 128), jnp.float32),
            coarse_slabs(), coarse_slabs(), coarse_slabs(),
            dma((4, 2)),
            dma((n_rim,)), dma((n_rim,)),
            dma((n_near,)), dma((n_near,)),
            dma((n_near,)), dma((n_near,)),
            dma((n_near,)), dma((n_near,)),
            dma((n_ring,)), dma((n_ring,)),
            pltpu.SemaphoreType.REGULAR((len(NEAR),)),
        ],
        compiler_params=pltpu.CompilerParams(collective_id=0, has_side_effects=True, vmem_limit_bytes=48 * 2**20),
        name="cycle",
    )(*[pltpu.with_memory_space_constraint(v, pltpu.HBM) for v in (source, guess, mass_coef, diffusion)])


def solution(mesh):
    spec = P("box", "sub", None)
    return jax.shard_map(body, mesh=mesh, in_specs=(spec,) * 4, out_specs=spec, check_vma=False)
```

```python
import functools

import jax
import jax.numpy as jnp
from jax import lax
from jax.experimental import pallas as pl
from jax.experimental.pallas import tpu as pltpu
from jax.sharding import PartitionSpec as P

MESH = pl.DeviceIdType.MESH
CHEB_C = 8
FINE_LOW = 0.25
FINE_HIGH = 2.0
COARSE_LOW = 0.05
COARSE_HIGH = 2.0

FX0, FX1, FR0, FRN = 3, 7, 4, 32
CX0, CR0, CRN = 4, 4, 16
GUESS, DIFF, SOURCE, MASS = 0, 1, 2, 3

NEAR = [(i, j) for i in (-2, 2, -1, 1) for j in (-1, 1)] + [(-2, 0), (2, 0), (0, -1), (0, 1), (-1, 0), (1, 0)]
BESIDE = [o for o in NEAR if abs(o[0]) < 2]
LOW_Y, LOW_Z, LOW_X, ROOT = (0, 6), (1, 7), (2, 5), (3, 4)
C_SLOTS, A_SLOTS, B_SLOTS = 8, 2, 4
STEP, ITERATE = (0, 3), (1, 2)
RING = [(i, j) for i in (-1, 1) for j in (-1, 1)] + [(0, -1), (0, 1), (-1, 0), (1, 0)]


def cheb_coeffs(count_steps, low_end, high_end):
    center_val = (high_end + low_end) / 2.0
    half_width = (high_end - low_end) / 2.0
    sigma_val = center_val / half_width
    factor_prev = 1.0 / sigma_val
    coeffs_list = [(0.0, 1.0 / center_val)]
    for number in range(1, count_steps):
        factor_next = 1.0 / (2.0 * sigma_val - factor_prev)
        coeffs_list.append((factor_next * factor_prev, 2.0 * factor_next / half_width))
        factor_prev = factor_next
    return coeffs_list


def coarse_rows(os, width):
    if os == 1:
        return pl.ds(CR0 + CRN - width, width), pl.ds(CR0 - width, width)
    if os == -1:
        return pl.ds(CR0, width), pl.ds(CR0 + CRN, width)
    return pl.ds(CR0, CRN), pl.ds(CR0, CRN)


def coef_cut(o):
    return {2: (3, 5), -2: (0, 6)}.get(o[0], (0, C_SLOTS)) + (2 if abs(o[0]) == 2 else 4,)


def rhs_cut(o):
    if abs(o[0]) == 2 and o[1] != 0:
        return (1 if o[0] == 2 else 0), 1, 1
    return 0, A_SLOTS, (4 if o[0] == 0 else 3)


def iterate_cut(o):
    return {2: (1, 3), -2: (0, 3)}.get(o[0], (0, B_SLOTS)) + (2 if abs(o[0]) == 2 else 4,)


def fine_cut(o, start, size, width):
    if o == 1:
        return pl.ds(start + size - width, width), pl.ds(start - width, width)
    if o == -1:
        return pl.ds(start, width), pl.ds(start + size, width)
    return pl.ds(start, size), pl.ds(start, size)


def rim_messages():
    own_x, own_rows, all_four = pl.ds(FX0, 4), pl.ds(FR0, FRN), pl.ds(0, 4)
    beside = []
    for j in (-1, 1):
        beside.append(((0, j), all_four, own_x, own_x) + fine_cut(j, FR0, FRN, 3))
    for i in (-1, 1):
        for j in (-1, 1):
            beside.append(((i, j), all_four) + fine_cut(i, FX0, 4, 2) + fine_cut(j, FR0, FRN, 2))
    ranks = []
    for depth in range(3):
        arrays = all_four if depth < 2 else pl.ds(0, 2)
        ranks.append([
            ((-1, 0), arrays, pl.ds(FX0 + depth, 1), pl.ds(FX1 + depth, 1), own_rows, own_rows),
            ((1, 0), arrays, pl.ds(FX1 - 1 - depth, 1), pl.ds(FX0 - 1 - depth, 1), own_rows, own_rows)])
    return [beside] + ranks


def dot(a, b):
    return jnp.dot(a, b, precision=lax.Precision.HIGHEST, preferred_element_type=jnp.float32)


def kernel(source, guess, mass, diff, out, F, FX, FY, FZ, DIAG, INV, W1, W2, DIR, RES, L2, C, G, A, B, XA, XB, CD, SPREAD,
           load_sem, r_send, r_recv, c_send, c_recv, e_send, e_recv, b_send, b_recv, l_send, l_recv, ready):
    f32 = jnp.float32
    nbox, nsub = lax.axis_size("box"), lax.axis_size("sub")
    b, s = lax.axis_index("box"), lax.axis_index("sub")

    def both(p, q):
        return jnp.logical_and(p, q)

    def exists(o):
        box_in = {-2: b > 1, -1: b > 0, 0: None, 1: b < nbox - 1, 2: b < nbox - 2}[o[0]]
        sub_in = {-1: s > 0, 0: None, 1: s < nsub - 1}[o[1]]
        if box_in is None or sub_in is None:
            return sub_in if box_in is None else box_in
        return both(box_in, sub_in)

    inner = both(both(b > 1, b < nbox - 2), both(s > 0, s < nsub - 1))
    rim = jnp.logical_not(inner)

    def each(messages, act, back):
        @pl.when(inner)
        def _():
            for _, message in messages:
                act(message)

        @pl.when(rim)
        def _():
            for o, message in messages:
                pl.when(exists((-o[0], -o[1]) if back else o))(functools.partial(act, message))

    def start(messages):
        each(messages, lambda m: m.start(), False)

    def arrived(messages):
        each(messages, lambda m: m.wait_recv(), True)

    def left(messages):
        each(messages, lambda m: m.wait_send(), False)

    def message(o, src, dst, send, recv):
        return o, pltpu.make_async_remote_copy(
            src_ref=src, dst_ref=dst, send_sem=send, recv_sem=recv, device_id=(b + o[0], s + o[1]), device_id_type=MESH)

    loads = []
    for k, ref in enumerate((guess, diff, source, mass)):
        for h in range(2):
            loads.append(pltpu.make_async_copy(
                ref.at[:, :, pl.ds(128 * h, 128)], F.at[k, pl.ds(FX0, 4), h, pl.ds(FR0, FRN)], load_sem.at[k, h]))
            loads[-1].start()
    barrier = pltpu.get_barrier_semaphore()

    def greet(o, semaphore):
        pl.semaphore_signal(semaphore, inc=1, device_id=(b + o[0], s + o[1]), device_id_type=MESH)

    def minus(o):
        return (-o[0], -o[1])

    origin = both(b == 0, s == 0)
    other = jnp.logical_not(origin)

    def is_origin(o):
        return both(b + o[0] == 0, s + o[1] == 0)

    def there(o):
        return both(exists(o), jnp.logical_not(is_origin(o)))

    for o in BESIDE:
        pl.when(both(exists(o), other))(functools.partial(greet, o, barrier))
    for o in NEAR:
        if abs(o[0]) == 2:
            pl.when(is_origin(o))(functools.partial(greet, o, barrier))
    def outside(x_cut, row_cut, X_cut, coarse_row_cut, n_x, n_rows, n_X, n_coarse_rows):
        F[0:3, x_cut, :, row_cut] = jnp.zeros((3, n_x, 2, n_rows, 128), f32)
        F[3:4, x_cut, :, row_cut] = jnp.ones((1, n_x, 2, n_rows, 128), f32)
        L2[x_cut, :, row_cut] = jnp.zeros((n_x, 2, n_rows, 128), f32)
        blank_coarse(X_cut, coarse_row_cut, n_X, n_coarse_rows)

    def blank_coarse(group_cut, row_cut, n_groups, n_rows):
        for ref, slots in ((C, C_SLOTS), (A, A_SLOTS), (B, B_SLOTS)):
            ref[group_cut, :, row_cut] = jnp.zeros((n_groups, slots, n_rows, 128), f32)

    def blank():
        every = slice(None)
        pl.when(b == 0)(lambda: outside(slice(0, FX0), every, slice(0, 2), every, FX0, 40, 2, 24))
        pl.when(b == nbox - 1)(lambda: outside(slice(FX1, 10), every, slice(3, 5), every, 10 - FX1, 40, 2, 24))
        pl.when(s == 0)(lambda: outside(every, slice(0, 4), every, slice(0, 4), 10, 4, 5, 4))
        pl.when(s == nsub - 1)(lambda: outside(every, slice(36, 40), every, slice(20, 24), 10, 4, 5, 4))
        pl.when(b == 1)(lambda: blank_coarse(slice(0, 1), every, 1, 24))
        pl.when(b == nbox - 2)(lambda: blank_coarse(slice(4, 5), every, 1, 24))

    first, k = [], 0
    for group in rim_messages():
        first.append([])
        for o, arrays, xs, xd, rs, rd in group:
            first[-1].append(message(o, F.at[arrays, xs, :, rs], F.at[arrays, xd, :, rd], r_send.at[k], r_recv.at[k]))
            k += 1
    flat = [m for group in first for m in group]
    n_sub = jnp.minimum(s, 1) + jnp.minimum(nsub - 1 - s, 1)
    n_beside = (jnp.minimum(b, 1) + jnp.minimum(nbox - 1 - b, 1) + 1) * (n_sub + 1) - 1
    n_near = (jnp.minimum(b, 2) + jnp.minimum(nbox - 1 - b, 2) + 1) * (n_sub + 1) - 1
    by_origin = both(both(b < 2, s < 2), other)

    def wait_barrier(count):
        pl.when(count > 0)(lambda: pl.semaphore_wait(barrier, count))

    pl.when(origin)(lambda: wait_barrier(n_near))
    pl.when(by_origin)(lambda: wait_barrier(n_beside - 1))
    pl.when(jnp.logical_not(jnp.logical_or(origin, by_origin)))(lambda: wait_barrier(n_beside))

    def slot(o):
        return ready.at[NEAR.index(o)]

    @pl.when(origin)
    def _():
        for o in NEAR:
            if o[0] >= 0 and o[1] >= 0:
                pl.when(exists(o))(functools.partial(greet, o, slot(minus(o))))

    for load in loads:
        load.wait()

    def send(o):
        for m in flat:
            if m[0] == o:
                m[1].start()

    def send_met(o):
        pl.semaphore_wait(slot(o), 1)
        send(o)

    @pl.when(inner)
    def _():
        for _, m in flat:
            m.start()

    @pl.when(rim)
    def _():
        for o in BESIDE:
            pl.when(there(o))(functools.partial(send, o))
        for o in BESIDE:
            if o[0] <= 0 and o[1] <= 0:
                pl.when(is_origin(o))(functools.partial(send_met, o))
    pl.when(rim)(blank)

    lane = lax.broadcasted_iota(jnp.int32, (256, 128), 0)
    cell = lax.broadcasted_iota(jnp.int32, (256, 128), 1)
    z_mean = jnp.where(lax.shift_right_logical(lane, 1) == cell, f32(0.5), f32(0.0))
    z_low = jnp.where(lax.shift_right_logical(lane + 1, 1) == cell, f32(0.5), f32(0.0))
    z_high = jnp.where(lax.shift_right_logical(lane + 1, 1) == cell + 1, f32(0.5), f32(0.0))
    row = lax.broadcasted_iota(jnp.int32, (2, 40, 128), 1)
    row_in = jnp.logical_and(jnp.logical_or(row >= FR0, s > 0), jnp.logical_or(row < FR0 + FRN, s < nsub - 1))
    row_mask = jnp.where(row_in, f32(1.0), f32(0.0))
    lane_f = lax.broadcasted_iota(jnp.int32, (2, 40, 128), 2)
    half = lax.broadcasted_iota(jnp.int32, (2, 40, 128), 0)
    z_first = jnp.logical_and(lane_f == 0, half == 0)
    z_last = jnp.logical_and(lane_f == 127, half == 1)

    def shift(v, edge, by):
        r = pltpu.roll(v, by, 2)
        return jnp.where(edge, jnp.stack([r[1], r[0]]), r)

    def from_below(v):
        return shift(v, lane_f == 0, 1)

    def from_above(v):
        return shift(v, lane_f == 127, 127)


    def slab_in(x):
        inside = jnp.logical_and(jnp.logical_or(x >= FX0, b > 0), jnp.logical_or(x < FX1, b < nbox - 1))
        return jnp.where(inside, f32(1.0), f32(0.0))

    def face(x):
        FX[x] = 0.5 * (F[DIFF, x - 1] + F[DIFF, x])

    def operator(x):
        d = F[DIFF, x]
        fy = 0.5 * (d + pltpu.roll(d, 1, 1))
        fz = 0.5 * (d + jnp.where(z_first, f32(0.0), from_below(d)))
        fz_high = 0.5 * (d + jnp.where(z_last, f32(0.0), from_above(d)))
        diag = F[MASS, x] + FX[x] + FX[x + 1] + fy + pltpu.roll(fy, 39, 1) + fz + fz_high
        FY[x] = fy
        FZ[x] = jnp.where(z_first, f32(0.0), fz)
        DIAG[x] = diag
        INV[x] = (row_mask * slab_in(x)) / diag

    def defect(u_ref, x):
        u = u_ref[x]
        fy, fz = FY[x], FZ[x]
        around = FX[x] * u_ref[x - 1] + FX[x + 1] * u_ref[x + 1]
        around = around + fy * pltpu.roll(u, 1, 1) + pltpu.roll(fy * u, 39, 1)
        around = around + fz * from_below(u) + from_above(fz * u)
        return (F[SOURCE, x] - DIAG[x] * u) + around, u

    fine = cheb_coeffs(2, FINE_LOW, FINE_HIGH)
    coarse = cheb_coeffs(CHEB_C, COARSE_LOW, COARSE_HIGH)

    def first_step(u_ref, to_ref, x):
        c, u = defect(u_ref, x)
        step_dir = (fine[0][1] * INV[x]) * c
        DIR[x] = step_dir
        to_ref[x] = u + step_dir

    def second_step(x):
        c, u = defect(W1, x)
        return u + (fine[1][0] * DIR[x] + (fine[1][1] * INV[x]) * c)

    def over(lo, hi, work, step=1):
        def turn(k, carry):
            work(lo + step * k)
            return carry

        lax.fori_loop(0, (hi - lo + step - 1) // step, turn, 0, unroll=True)

    def with_operator(x):
        operator(x)
        first_step(F.at[GUESS], W1, x)

    def smooth(x):
        W2[x] = second_step(x)

    def find_residual(x):
        RES[x] = defect(W2, x)[0]

    arrived(first[0])
    over(4, 7, face)
    arrived(first[1])
    def rows(ref, x, start):
        return ref[x, :, pl.ds(start, 16, 2), :]

    def wide(parts):
        return jnp.concatenate([jnp.concatenate([v[0], v[1]], 1) for v in parts], 0)


    D, M = F.at[DIFF], F.at[MASS]
    pair = {x: rows(D, x, FR0) + rows(D, x, FR0 + 1) for x in range(FX0 - 1, FX1 + 1)}
    low_y = {x: rows(D, x, FR0 - 1) + rows(D, x, FR0) for x in range(FX0, FX1)}
    high_y = {x: rows(D, x, FR0 + 1) + rows(D, x, FR0 + 2) for x in range(FX0, FX1)}
    in_mean, in_z = [], []
    for X in range(2):
        x = FX0 + 2 * X
        face_low, face_high = 0.25 * (pair[x - 1] + pair[x]), 0.25 * (pair[x + 1] + pair[x + 2])
        y_low, y_high = 0.25 * (low_y[x] + low_y[x + 1]), 0.25 * (high_y[x] + high_y[x + 1])
        mean_mass = 0.25 * (rows(M, x, FR0) + rows(M, x, FR0 + 1) + rows(M, x + 1, FR0) + rows(M, x + 1, FR0 + 1))
        in_mean += [face_low, y_low, mean_mass + 0.25 * (face_low + face_high + y_low + y_high)]
        in_z.append(0.25 * (pair[x] + pair[x + 1]))
    means = dot(wide(in_mean), z_mean)
    over_z = wide(in_z)
    lows_z, highs_z = dot(over_z, z_low), dot(over_z, z_high)
    own_s = []
    for X in range(2):
        fx, fy, d = (means[(3 * X + k) * 16:(3 * X + k + 1) * 16] for k in range(3))
        fz = lows_z[16 * X:16 * X + 16]
        d = d + 0.25 * (fz + highs_z[16 * X:16 * X + 16])
        sc = lax.rsqrt(d)
        sc = sc * (1.5 - 0.5 * d * sc * sc)
        own_s.append(sc)
        for kind, v in ((LOW_X, fx), (LOW_Y, fy), (LOW_Z, fz), (ROOT, sc)):
            C[2, kind[X], pl.ds(CR0, CRN), :] = v

    def coarse_messages(src, cut, sends, recvs):
        found = []
        for k, o in enumerate(NEAR):
            at, count, width = cut(o)
            rs, rd = coarse_rows(o[1], width)
            found.append(message(
                o, src.at[2, pl.ds(at, count), rs], src.at[2 - o[0], pl.ds(at, count), rd], sends.at[k], recvs.at[k]))
        start(found)
        return found

    def meet(o):
        pl.semaphore_wait(slot(o), 1)

    for o in ((-2, 0), (-2, -1)):
        pl.when(is_origin(o))(functools.partial(meet, o))
    coefs = coarse_messages(C, coef_cut, c_send, c_recv)

    over(3, 8, face, 4)
    over(3, 7, with_operator)
    arrived(first[2])
    over(2, 9, face, 6)
    over(2, 8, with_operator, 5)
    over(3, 7, smooth)
    arrived(first[3])
    over(1, 10, face, 8)
    over(1, 9, with_operator, 7)
    over(2, 8, smooth, 5)
    over(FX0, FX1, find_residual)

    means = []
    for X in range(2):
        x = FX0 + 2 * X
        means.append(0.25 * ((rows(RES, x, FR0) + rows(RES, x, FR0 + 1)) + (rows(RES, x + 1, FR0) + rows(RES, x + 1, FR0 + 1))))
    rhs = dot(wide(means), z_mean)
    for X in range(2):
        A[2, X, pl.ds(CR0, CRN), :] = own_s[X] * rhs[16 * X:16 * X + 16]
    e_one = coarse_messages(A, rhs_cut, e_send, e_recv)

    for x in range(FX0 - 1, FX1 + 1):
        L2[x, :, pl.ds(FR0, FRN), :] = W2[x, :, pl.ds(FR0, FRN), :]
    late = []
    for k, o in enumerate(RING):
        if o[1] == 0:
            at_x = FX1 - 2 if o[0] == 1 else FX0 + 1
            xs, xd = pl.ds(at_x, 1), pl.ds(at_x - 4 * o[0], 1)
        else:
            xs, xd = fine_cut(o[0], FX0, 4, 1)
        rs, rd = fine_cut(o[1], FR0, FRN, 2 if o[0] == 0 else 1)
        late.append(message(o, L2.at[xs, :, rs], L2.at[xd, :, rd], l_send.at[k], l_recv.at[k]))
    start(late)

    arrived(coefs)
    clane = lax.broadcasted_iota(jnp.int32, (24, 128), 1)

    def coef(kind, X):
        return C[X // 2, kind[X % 2]]

    for X in range(1, 10):
        sc = coef(ROOT, X)
        G[0, X] = coef(LOW_X, X) * ((0.25 * sc) * coef(ROOT, X - 1))
        if X < 9:
            G[1, X] = coef(LOW_Y, X) * ((0.25 * sc) * pltpu.roll(sc, 1, 0))
            G[2, X] = jnp.where(clane == 0, f32(0.0), coef(LOW_Z, X) * ((0.25 * sc) * pltpu.roll(sc, 1, 1)))

    def coarse_step(iterate, step_of, X, number):
        keep, gain = coarse[number]
        x = iterate(X)
        gy, gz = G[1, X], G[2, X]
        c = (A[X // 2, X % 2] - x) + G[0, X] * iterate(X - 1) + G[0, X + 1] * iterate(X + 1)
        c = c + gy * pltpu.roll(x, 1, 0) + pltpu.roll(gy * x, 23, 0)
        c = c + gz * pltpu.roll(x, 1, 1) + pltpu.roll(gz * x, 127, 1)
        step_dir = keep * step_of(X) + gain * c
        return x + step_dir, step_dir

    left(flat)
    arrived(e_one)
    for X in range(10):
        begin = coarse[0][1] * A[X // 2, X % 2]
        XA[X] = begin
        CD[X] = begin

    def of(ref):
        return lambda X: ref[X]

    now, later = XA, XB
    for number in range(1, 4):
        for X in range(number, 10 - number):
            later[X], CD[X] = coarse_step(of(now), of(CD), X, number)
        now, later = later, now
    for X in range(CX0, CX0 + 2):
        new_x, new_d = coarse_step(of(now), of(CD), X, 4)
        B[2, ITERATE[X % 2], pl.ds(CR0, CRN), :] = new_x[CR0:CR0 + CRN]
        B[2, STEP[X % 2], pl.ds(CR0, CRN), :] = new_d[CR0:CR0 + CRN]
    e_two = coarse_messages(B, iterate_cut, b_send, b_recv)
    left(coefs + e_one)
    arrived(late)
    left(late)
    arrived(e_two)
    iterate, step_of = (lambda X: B[X // 2, ITERATE[X % 2]]), (lambda X: B[X // 2, STEP[X % 2]])
    for number, later in ((5, XA), (6, XB), (7, XA)):
        for X in range(number - 4, 14 - number):
            later[X], CD[X] = coarse_step(iterate, step_of, X, number)
        iterate, step_of = of(later), of(CD)

    spread_z = jnp.where(
        lax.shift_right_logical(lax.broadcasted_iota(jnp.int32, (128, 256), 1), 1) == lax.broadcasted_iota(jnp.int32, (128, 256), 0),
        f32(1.0), f32(0.0))
    corr = dot(jnp.concatenate([coef(ROOT, X) * iterate(X) for X in range(3, 7)], 0), spread_z)
    for X in range(4):
        for h in range(2):
            part = corr[24 * X:24 * X + 24, 128 * h:128 * h + 128]
            SPREAD[X, h, pl.ds(0, 24, 2), :] = part
            SPREAD[X, h, pl.ds(1, 24, 2), :] = part
    for x in range(1, 9):
        W2[x] = L2[x] + SPREAD[(x - 1) // 2, :, pl.ds(2 * CR0 - FR0, 40), :]

    over(2, 8, functools.partial(first_step, W2, W1))
    for x in range(FX0, FX1):
        last = second_step(x)
        for h in range(2):
            out[x - FX0, :, 128 * h:128 * h + 128] = last[h, FR0:FR0 + FRN]

    left(e_two)


def body(source, guess, mass_coef, diffusion):
    vmem = pltpu.VMEM
    fine_slabs = lambda: vmem((10, 2, 40, 128), jnp.float32)
    coarse_slabs = lambda: vmem((10, 24, 128), jnp.float32)
    n_rim, n_near, n_ring = sum(len(group) for group in rim_messages()), len(NEAR), len(RING)
    dma = pltpu.SemaphoreType.DMA
    return pl.pallas_call(
        kernel,
        out_shape=jax.ShapeDtypeStruct((4, 32, 256), jnp.float32),
        in_specs=[pl.BlockSpec(memory_space=pltpu.HBM)] * 4,
        out_specs=pl.BlockSpec(memory_space=pltpu.VMEM),
        scratch_shapes=[
            vmem((4, 10, 2, 40, 128), jnp.float32),
            fine_slabs(), fine_slabs(), fine_slabs(), fine_slabs(), fine_slabs(),
            fine_slabs(), fine_slabs(), fine_slabs(), fine_slabs(), fine_slabs(),
            vmem((5, C_SLOTS, 24, 128), jnp.float32),
            vmem((3, 10, 24, 128), jnp.float32),
            vmem((5, A_SLOTS, 24, 128), jnp.float32),
            vmem((5, B_SLOTS, 24, 128), jnp.float32),
            coarse_slabs(), coarse_slabs(), coarse_slabs(),
            vmem((4, 2, 48, 128), jnp.float32),
            dma((4, 2)),
            dma((n_rim,)), dma((n_rim,)),
            dma((n_near,)), dma((n_near,)),
            dma((n_near,)), dma((n_near,)),
            dma((n_near,)), dma((n_near,)),
            dma((n_ring,)), dma((n_ring,)),
            pltpu.SemaphoreType.REGULAR((len(NEAR),)),
        ],
        compiler_params=pltpu.CompilerParams(collective_id=0, has_side_effects=True, vmem_limit_bytes=48 * 2**20),
        name="cycle",
    )(*[pltpu.with_memory_space_constraint(v, pltpu.HBM) for v in (source, guess, mass_coef, diffusion)])


def solution(mesh):
    spec = P("box", "sub", None)
    return jax.shard_map(body, mesh=mesh, in_specs=(spec,) * 4, out_specs=spec, check_vma=False)
```

```python
import functools

import jax
import jax.numpy as jnp
from jax import lax
from jax.experimental import pallas as pl
from jax.experimental.pallas import tpu as pltpu
from jax.sharding import PartitionSpec as P

MESH = pl.DeviceIdType.MESH
CHEB_C = 8
FINE_LOW = 0.25
FINE_HIGH = 2.0
COARSE_LOW = 0.05
COARSE_HIGH = 2.0

FX0, FX1, FR0, FRN = 3, 7, 4, 32
CX0, CR0, CRN = 4, 4, 16
GUESS, DIFF, SOURCE, MASS = 0, 1, 2, 3

NEAR = [(i, j) for i in (-2, 2, -1, 1) for j in (-1, 1)] + [(-2, 0), (2, 0), (0, -1), (0, 1), (-1, 0), (1, 0)]
BESIDE = [o for o in NEAR if abs(o[0]) < 2]
LOW_Y, LOW_Z, LOW_X, ROOT = (0, 6), (1, 7), (2, 5), (3, 4)
C_SLOTS, A_SLOTS, B_SLOTS = 8, 2, 4
STEP, ITERATE = (0, 3), (1, 2)
RING = [(i, j) for i in (-1, 1) for j in (-1, 1)] + [(0, -1), (0, 1), (-1, 0), (1, 0)]


def cheb_coeffs(count_steps, low_end, high_end):
    center_val = (high_end + low_end) / 2.0
    half_width = (high_end - low_end) / 2.0
    sigma_val = center_val / half_width
    factor_prev = 1.0 / sigma_val
    coeffs_list = [(0.0, 1.0 / center_val)]
    for number in range(1, count_steps):
        factor_next = 1.0 / (2.0 * sigma_val - factor_prev)
        coeffs_list.append((factor_next * factor_prev, 2.0 * factor_next / half_width))
        factor_prev = factor_next
    return coeffs_list


def coarse_rows(os, width):
    if os == 1:
        return pl.ds(CR0 + CRN - width, width), pl.ds(CR0 - width, width)
    if os == -1:
        return pl.ds(CR0, width), pl.ds(CR0 + CRN, width)
    return pl.ds(CR0, CRN), pl.ds(CR0, CRN)


def coef_cut(o):
    return {2: (3, 5), -2: (0, 6)}.get(o[0], (0, C_SLOTS)) + (2 if abs(o[0]) == 2 else 4,)


def rhs_cut(o):
    if abs(o[0]) == 2 and o[1] != 0:
        return (1 if o[0] == 2 else 0), 1, 1
    return 0, A_SLOTS, (4 if o[0] == 0 else 3)


def iterate_cut(o):
    return {2: (1, 3), -2: (0, 3)}.get(o[0], (0, B_SLOTS)) + (2 if abs(o[0]) == 2 else 4,)


def fine_cut(o, start, size, width):
    if o == 1:
        return pl.ds(start + size - width, width), pl.ds(start - width, width)
    if o == -1:
        return pl.ds(start, width), pl.ds(start + size, width)
    return pl.ds(start, size), pl.ds(start, size)


def rim_messages():
    own_x, own_rows, all_four = pl.ds(FX0, 4), pl.ds(FR0, FRN), pl.ds(0, 4)
    beside = []
    for j in (-1, 1):
        beside.append(((0, j), all_four, own_x, own_x) + fine_cut(j, FR0, FRN, 3))
    for i in (-1, 1):
        for j in (-1, 1):
            beside.append(((i, j), all_four) + fine_cut(i, FX0, 4, 2) + fine_cut(j, FR0, FRN, 2))
    ranks = []
    for depth in range(3):
        arrays = all_four if depth < 2 else pl.ds(0, 2)
        ranks.append([
            ((-1, 0), arrays, pl.ds(FX0 + depth, 1), pl.ds(FX1 + depth, 1), own_rows, own_rows),
            ((1, 0), arrays, pl.ds(FX1 - 1 - depth, 1), pl.ds(FX0 - 1 - depth, 1), own_rows, own_rows)])
    return [beside] + ranks


def dot(a, b):
    bf16 = jnp.bfloat16
    high = a.astype(bf16)
    rest = a - high.astype(jnp.float32)
    middle = rest.astype(bf16)
    low = (rest - middle.astype(jnp.float32)).astype(bf16)
    parts = jnp.dot(jnp.concatenate([low, middle, high], 0), b.astype(bf16), preferred_element_type=jnp.float32)
    n = a.shape[0]
    return (parts[:n] + parts[n:2 * n]) + parts[2 * n:]


def kernel(source, guess, mass, diff, out, F, FX, FY, FZ, DIAG, INV, W1, W2, DIR, RES, L2, C, G, A, B, XA, XB, CD, SPREAD,
           load_sem, r_send, r_recv, c_send, c_recv, e_send, e_recv, b_send, b_recv, l_send, l_recv, ready):
    f32 = jnp.float32
    nbox, nsub = lax.axis_size("box"), lax.axis_size("sub")
    b, s = lax.axis_index("box"), lax.axis_index("sub")

    def both(p, q):
        return jnp.logical_and(p, q)

    def exists(o):
        box_in = {-2: b > 1, -1: b > 0, 0: None, 1: b < nbox - 1, 2: b < nbox - 2}[o[0]]
        sub_in = {-1: s > 0, 0: None, 1: s < nsub - 1}[o[1]]
        if box_in is None or sub_in is None:
            return sub_in if box_in is None else box_in
        return both(box_in, sub_in)

    inner = both(both(b > 1, b < nbox - 2), both(s > 0, s < nsub - 1))
    rim = jnp.logical_not(inner)

    def each(messages, act, back):
        @pl.when(inner)
        def _():
            for _, message in messages:
                act(message)

        @pl.when(rim)
        def _():
            for o, message in messages:
                pl.when(exists((-o[0], -o[1]) if back else o))(functools.partial(act, message))

    def start(messages):
        each(messages, lambda m: m.start(), False)

    def arrived(messages):
        each(messages, lambda m: m.wait_recv(), True)

    def left(messages):
        each(messages, lambda m: m.wait_send(), False)

    def message(o, src, dst, send, recv):
        return o, pltpu.make_async_remote_copy(
            src_ref=src, dst_ref=dst, send_sem=send, recv_sem=recv, device_id=(b + o[0], s + o[1]), device_id_type=MESH)

    barrier = pltpu.get_barrier_semaphore()

    def greet(o, semaphore):
        pl.semaphore_signal(semaphore, inc=1, device_id=(b + o[0], s + o[1]), device_id_type=MESH)

    def minus(o):
        return (-o[0], -o[1])

    origin = both(b == 0, s == 0)
    other = jnp.logical_not(origin)

    def is_origin(o):
        return both(b + o[0] == 0, s + o[1] == 0)

    def there(o):
        return both(exists(o), jnp.logical_not(is_origin(o)))

    n_sub = jnp.minimum(s, 1) + jnp.minimum(nsub - 1 - s, 1)
    n_beside = (jnp.minimum(b, 1) + jnp.minimum(nbox - 1 - b, 1) + 1) * (n_sub + 1) - 1
    n_near = (jnp.minimum(b, 2) + jnp.minimum(nbox - 1 - b, 2) + 1) * (n_sub + 1) - 1

    def wait_barrier(count):
        pl.when(count > 0)(lambda: pl.semaphore_wait(barrier, count))

    def slot(o):
        return ready.at[NEAR.index(o)]

    @pl.when(origin)
    def _():
        wait_barrier(n_near)
        for o in NEAR:
            if o[0] >= 0 and o[1] >= 0:
                pl.when(exists(o))(functools.partial(greet, o, slot(minus(o))))

    loads = []
    for k, ref in enumerate((guess, diff, source, mass)):
        for h in range(2):
            loads.append(pltpu.make_async_copy(
                ref.at[:, :, pl.ds(128 * h, 128)], F.at[k, pl.ds(FX0, 4), h, pl.ds(FR0, FRN)], load_sem.at[k, h]))
            loads[-1].start()
    for o in BESIDE:
        pl.when(both(exists(o), other))(functools.partial(greet, o, barrier))
    for o in NEAR:
        if abs(o[0]) == 2:
            pl.when(is_origin(o))(functools.partial(greet, o, barrier))
    def outside(x_cut, row_cut, X_cut, coarse_row_cut, n_x, n_rows, n_X, n_coarse_rows):
        F[0:3, x_cut, :, row_cut] = jnp.zeros((3, n_x, 2, n_rows, 128), f32)
        F[3:4, x_cut, :, row_cut] = jnp.ones((1, n_x, 2, n_rows, 128), f32)
        L2[x_cut, :, row_cut] = jnp.zeros((n_x, 2, n_rows, 128), f32)
        blank_coarse(X_cut, coarse_row_cut, n_X, n_coarse_rows)

    def blank_coarse(group_cut, row_cut, n_groups, n_rows):
        for ref, slots in ((C, C_SLOTS), (A, A_SLOTS), (B, B_SLOTS)):
            ref[group_cut, :, row_cut] = jnp.zeros((n_groups, slots, n_rows, 128), f32)

    def blank():
        every = slice(None)
        pl.when(b == 0)(lambda: outside(slice(0, FX0), every, slice(0, 2), every, FX0, 40, 2, 24))
        pl.when(b == nbox - 1)(lambda: outside(slice(FX1, 10), every, slice(3, 5), every, 10 - FX1, 40, 2, 24))
        pl.when(s == 0)(lambda: outside(every, slice(0, 4), every, slice(0, 4), 10, 4, 5, 4))
        pl.when(s == nsub - 1)(lambda: outside(every, slice(36, 40), every, slice(20, 24), 10, 4, 5, 4))
        pl.when(b == 1)(lambda: blank_coarse(slice(0, 1), every, 1, 24))
        pl.when(b == nbox - 2)(lambda: blank_coarse(slice(4, 5), every, 1, 24))

    first, k = [], 0
    for group in rim_messages():
        first.append([])
        for o, arrays, xs, xd, rs, rd in group:
            first[-1].append(message(o, F.at[arrays, xs, :, rs], F.at[arrays, xd, :, rd], r_send.at[k], r_recv.at[k]))
            k += 1
    flat = [m for group in first for m in group]
    by_origin = both(both(b < 2, s < 2), other)

    pl.when(by_origin)(lambda: wait_barrier(n_beside - 1))
    pl.when(jnp.logical_not(jnp.logical_or(origin, by_origin)))(lambda: wait_barrier(n_beside))

    for load in loads:
        load.wait()

    def send(o):
        for m in flat:
            if m[0] == o:
                m[1].start()

    def send_met(o):
        pl.semaphore_wait(slot(o), 1)
        send(o)

    @pl.when(inner)
    def _():
        for _, m in flat:
            m.start()

    @pl.when(rim)
    def _():
        for o in BESIDE:
            pl.when(there(o))(functools.partial(send, o))
        for o in BESIDE:
            if o[0] <= 0 and o[1] <= 0:
                pl.when(is_origin(o))(functools.partial(send_met, o))
    pl.when(rim)(blank)

    lane = lax.broadcasted_iota(jnp.int32, (256, 128), 0)
    cell = lax.broadcasted_iota(jnp.int32, (256, 128), 1)
    z_mean = jnp.where(lax.shift_right_logical(lane, 1) == cell, f32(0.5), f32(0.0))
    z_low = jnp.where(lax.shift_right_logical(lane + 1, 1) == cell, f32(0.5), f32(0.0))
    z_high = jnp.where(lax.shift_right_logical(lane + 1, 1) == cell + 1, f32(0.5), f32(0.0))
    row = lax.broadcasted_iota(jnp.int32, (2, 40, 128), 1)
    row_in = jnp.logical_and(jnp.logical_or(row >= FR0, s > 0), jnp.logical_or(row < FR0 + FRN, s < nsub - 1))
    row_mask = jnp.where(row_in, f32(1.0), f32(0.0))
    lane_f = lax.broadcasted_iota(jnp.int32, (2, 40, 128), 2)
    half = lax.broadcasted_iota(jnp.int32, (2, 40, 128), 0)
    z_first = jnp.logical_and(lane_f == 0, half == 0)
    z_last = jnp.logical_and(lane_f == 127, half == 1)

    def shift(v, edge, by):
        r = pltpu.roll(v, by, 2)
        return jnp.where(edge, jnp.stack([r[1], r[0]]), r)

    def from_below(v):
        return shift(v, lane_f == 0, 1)

    def from_above(v):
        return shift(v, lane_f == 127, 127)


    def slab_in(x):
        inside = jnp.logical_and(jnp.logical_or(x >= FX0, b > 0), jnp.logical_or(x < FX1, b < nbox - 1))
        return jnp.where(inside, f32(1.0), f32(0.0))

    def face(x):
        FX[x] = 0.5 * (F[DIFF, x - 1] + F[DIFF, x])

    def operator(x):
        d = F[DIFF, x]
        fy = 0.5 * (d + pltpu.roll(d, 1, 1))
        fz = 0.5 * (d + jnp.where(z_first, f32(0.0), from_below(d)))
        fz_high = 0.5 * (d + jnp.where(z_last, f32(0.0), from_above(d)))
        diag = F[MASS, x] + FX[x] + FX[x + 1] + fy + pltpu.roll(fy, 39, 1) + fz + fz_high
        FY[x] = fy
        FZ[x] = jnp.where(z_first, f32(0.0), fz)
        DIAG[x] = diag
        INV[x] = (row_mask * slab_in(x)) / diag

    def defect(u_ref, x):
        u = u_ref[x]
        fy, fz = FY[x], FZ[x]
        around = FX[x] * u_ref[x - 1] + FX[x + 1] * u_ref[x + 1]
        around = around + fy * pltpu.roll(u, 1, 1) + pltpu.roll(fy * u, 39, 1)
        around = around + fz * from_below(u) + from_above(fz * u)
        return (F[SOURCE, x] - DIAG[x] * u) + around, u

    fine = cheb_coeffs(2, FINE_LOW, FINE_HIGH)
    coarse = cheb_coeffs(CHEB_C, COARSE_LOW, COARSE_HIGH)

    def first_step(u_ref, to_ref, x):
        c, u = defect(u_ref, x)
        step_dir = (fine[0][1] * INV[x]) * c
        DIR[x] = step_dir
        to_ref[x] = u + step_dir

    def second_step(x):
        c, u = defect(W1, x)
        return u + (fine[1][0] * DIR[x] + (fine[1][1] * INV[x]) * c)

    def over(lo, hi, work, step=1):
        def turn(k, carry):
            work(lo + step * k)
            return carry

        lax.fori_loop(0, (hi - lo + step - 1) // step, turn, 0, unroll=True)

    def with_operator(x):
        operator(x)
        first_step(F.at[GUESS], W1, x)

    def smooth(x):
        W2[x] = second_step(x)

    def find_residual(x):
        RES[x] = defect(W2, x)[0]

    arrived(first[0])
    over(4, 7, face)
    arrived(first[1])
    def rows(ref, x, start):
        return ref[x, :, pl.ds(start, 16, 2), :]

    def wide(parts):
        return jnp.concatenate([jnp.concatenate([v[0], v[1]], 1) for v in parts], 0)


    D, M = F.at[DIFF], F.at[MASS]
    pair = {x: rows(D, x, FR0) + rows(D, x, FR0 + 1) for x in range(FX0 - 1, FX1 + 1)}
    low_y = {x: rows(D, x, FR0 - 1) + rows(D, x, FR0) for x in range(FX0, FX1)}
    high_y = {x: rows(D, x, FR0 + 1) + rows(D, x, FR0 + 2) for x in range(FX0, FX1)}
    in_mean, in_z = [], []
    for X in range(2):
        x = FX0 + 2 * X
        face_low, face_high = 0.25 * (pair[x - 1] + pair[x]), 0.25 * (pair[x + 1] + pair[x + 2])
        y_low, y_high = 0.25 * (low_y[x] + low_y[x + 1]), 0.25 * (high_y[x] + high_y[x + 1])
        mean_mass = 0.25 * (rows(M, x, FR0) + rows(M, x, FR0 + 1) + rows(M, x + 1, FR0) + rows(M, x + 1, FR0 + 1))
        in_mean += [face_low, y_low, mean_mass + 0.25 * (face_low + face_high + y_low + y_high)]
        in_z.append(0.25 * (pair[x] + pair[x + 1]))
    means = dot(wide(in_mean), z_mean)
    over_z = wide(in_z)
    lows_z, highs_z = dot(over_z, z_low), dot(over_z, z_high)
    own_s = []
    for X in range(2):
        fx, fy, d = (means[(3 * X + k) * 16:(3 * X + k + 1) * 16] for k in range(3))
        fz = lows_z[16 * X:16 * X + 16]
        d = d + 0.25 * (fz + highs_z[16 * X:16 * X + 16])
        sc = lax.rsqrt(d)
        sc = sc * (1.5 - 0.5 * d * sc * sc)
        own_s.append(sc)
        for kind, v in ((LOW_X, fx), (LOW_Y, fy), (LOW_Z, fz), (ROOT, sc)):
            C[2, kind[X], pl.ds(CR0, CRN), :] = v

    def coarse_messages(src, cut, sends, recvs):
        found = []
        for k, o in enumerate(NEAR):
            at, count, width = cut(o)
            rs, rd = coarse_rows(o[1], width)
            found.append(message(
                o, src.at[2, pl.ds(at, count), rs], src.at[2 - o[0], pl.ds(at, count), rd], sends.at[k], recvs.at[k]))
        start(found)
        return found

    def meet(o):
        pl.semaphore_wait(slot(o), 1)

    for o in ((-2, 0), (-2, -1)):
        pl.when(is_origin(o))(functools.partial(meet, o))
    coefs = coarse_messages(C, coef_cut, c_send, c_recv)

    over(3, 8, face, 4)
    over(3, 7, with_operator)
    arrived(first[2])
    over(2, 9, face, 6)
    over(2, 8, with_operator, 5)
    over(3, 7, smooth)
    arrived(first[3])
    over(1, 10, face, 8)
    over(1, 9, with_operator, 7)
    over(2, 8, smooth, 5)
    over(FX0, FX1, find_residual)

    means = []
    for X in range(2):
        x = FX0 + 2 * X
        means.append(0.25 * ((rows(RES, x, FR0) + rows(RES, x, FR0 + 1)) + (rows(RES, x + 1, FR0) + rows(RES, x + 1, FR0 + 1))))
    rhs = dot(wide(means), z_mean)
    for X in range(2):
        A[2, X, pl.ds(CR0, CRN), :] = own_s[X] * rhs[16 * X:16 * X + 16]
    e_one = coarse_messages(A, rhs_cut, e_send, e_recv)

    for x in range(FX0 - 1, FX1 + 1):
        L2[x, :, pl.ds(FR0, FRN), :] = W2[x, :, pl.ds(FR0, FRN), :]
    late = []
    for k, o in enumerate(RING):
        if o[1] == 0:
            at_x = FX1 - 2 if o[0] == 1 else FX0 + 1
            xs, xd = pl.ds(at_x, 1), pl.ds(at_x - 4 * o[0], 1)
        else:
            xs, xd = fine_cut(o[0], FX0, 4, 1)
        rs, rd = fine_cut(o[1], FR0, FRN, 2 if o[0] == 0 else 1)
        late.append(message(o, L2.at[xs, :, rs], L2.at[xd, :, rd], l_send.at[k], l_recv.at[k]))
    start(late)

    arrived(coefs)
    clane = lax.broadcasted_iota(jnp.int32, (24, 128), 1)

    def coef(kind, X):
        return C[X // 2, kind[X % 2]]

    for X in range(1, 10):
        sc = coef(ROOT, X)
        G[0, X] = coef(LOW_X, X) * ((0.25 * sc) * coef(ROOT, X - 1))
        if X < 9:
            G[1, X] = coef(LOW_Y, X) * ((0.25 * sc) * pltpu.roll(sc, 1, 0))
            G[2, X] = jnp.where(clane == 0, f32(0.0), coef(LOW_Z, X) * ((0.25 * sc) * pltpu.roll(sc, 1, 1)))

    def coarse_step(iterate, step_of, X, number):
        keep, gain = coarse[number]
        x = iterate(X)
        gy, gz = G[1, X], G[2, X]
        c = (A[X // 2, X % 2] - x) + G[0, X] * iterate(X - 1) + G[0, X + 1] * iterate(X + 1)
        c = c + gy * pltpu.roll(x, 1, 0) + pltpu.roll(gy * x, 23, 0)
        c = c + gz * pltpu.roll(x, 1, 1) + pltpu.roll(gz * x, 127, 1)
        step_dir = keep * step_of(X) + gain * c
        return x + step_dir, step_dir

    left(flat)
    arrived(e_one)
    for X in range(10):
        begin = coarse[0][1] * A[X // 2, X % 2]
        XA[X] = begin
        CD[X] = begin

    def of(ref):
        return lambda X: ref[X]

    now, later = XA, XB
    for number in range(1, 4):
        for X in range(number, 10 - number):
            later[X], CD[X] = coarse_step(of(now), of(CD), X, number)
        now, later = later, now
    for X in range(CX0, CX0 + 2):
        new_x, new_d = coarse_step(of(now), of(CD), X, 4)
        B[2, ITERATE[X % 2], pl.ds(CR0, CRN), :] = new_x[CR0:CR0 + CRN]
        B[2, STEP[X % 2], pl.ds(CR0, CRN), :] = new_d[CR0:CR0 + CRN]
    e_two = coarse_messages(B, iterate_cut, b_send, b_recv)
    left(coefs + e_one)
    arrived(late)
    left(late)
    left(e_two)
    arrived(e_two)
    iterate, step_of = (lambda X: B[X // 2, ITERATE[X % 2]]), (lambda X: B[X // 2, STEP[X % 2]])
    for number, later in ((5, XA), (6, XB), (7, XA)):
        for X in range(number - 4, 14 - number):
            later[X], CD[X] = coarse_step(iterate, step_of, X, number)
        iterate, step_of = of(later), of(CD)

    spread_z = jnp.where(
        lax.shift_right_logical(lax.broadcasted_iota(jnp.int32, (128, 256), 1), 1) == lax.broadcasted_iota(jnp.int32, (128, 256), 0),
        f32(1.0), f32(0.0))
    corr = dot(jnp.concatenate([coef(ROOT, X) * iterate(X) for X in range(3, 7)], 0), spread_z)
    for X in range(4):
        for h in range(2):
            part = corr[24 * X:24 * X + 24, 128 * h:128 * h + 128]
            SPREAD[X, h, pl.ds(0, 24, 2), :] = part
            SPREAD[X, h, pl.ds(1, 24, 2), :] = part
    for x in range(1, 9):
        W2[x] = L2[x] + SPREAD[(x - 1) // 2, :, pl.ds(2 * CR0 - FR0, 40), :]

    over(2, 8, functools.partial(first_step, W2, W1))
    for x in range(FX0, FX1):
        last = second_step(x)
        for h in range(2):
            out[x - FX0, :, 128 * h:128 * h + 128] = last[h, FR0:FR0 + FRN]


def body(source, guess, mass_coef, diffusion):
    vmem = pltpu.VMEM
    fine_slabs = lambda: vmem((10, 2, 40, 128), jnp.float32)
    coarse_slabs = lambda: vmem((10, 24, 128), jnp.float32)
    n_rim, n_near, n_ring = sum(len(group) for group in rim_messages()), len(NEAR), len(RING)
    dma = pltpu.SemaphoreType.DMA
    return pl.pallas_call(
        kernel,
        out_shape=jax.ShapeDtypeStruct((4, 32, 256), jnp.float32),
        in_specs=[pl.BlockSpec(memory_space=pltpu.HBM)] * 4,
        out_specs=pl.BlockSpec(memory_space=pltpu.VMEM),
        scratch_shapes=[
            vmem((4, 10, 2, 40, 128), jnp.float32),
            fine_slabs(), fine_slabs(), fine_slabs(), fine_slabs(), fine_slabs(),
            fine_slabs(), fine_slabs(), fine_slabs(), fine_slabs(), fine_slabs(),
            vmem((5, C_SLOTS, 24, 128), jnp.float32),
            vmem((3, 10, 24, 128), jnp.float32),
            vmem((5, A_SLOTS, 24, 128), jnp.float32),
            vmem((5, B_SLOTS, 24, 128), jnp.float32),
            coarse_slabs(), coarse_slabs(), coarse_slabs(),
            vmem((4, 2, 48, 128), jnp.float32),
            dma((4, 2)),
            dma((n_rim,)), dma((n_rim,)),
            dma((n_near,)), dma((n_near,)),
            dma((n_near,)), dma((n_near,)),
            dma((n_near,)), dma((n_near,)),
            dma((n_ring,)), dma((n_ring,)),
            pltpu.SemaphoreType.REGULAR((len(NEAR),)),
        ],
        compiler_params=pltpu.CompilerParams(collective_id=0, has_side_effects=True, vmem_limit_bytes=48 * 2**20),
        name="cycle",
    )(*[pltpu.with_memory_space_constraint(v, pltpu.HBM) for v in (source, guess, mass_coef, diffusion)])


def solution(mesh):
    spec = P("box", "sub", None)
    return jax.shard_map(body, mesh=mesh, in_specs=(spec,) * 4, out_specs=spec, check_vma=False)
```

```python
import functools

import jax
import jax.numpy as jnp
from jax import lax
from jax.experimental import pallas as pl
from jax.experimental.pallas import tpu as pltpu
from jax.sharding import PartitionSpec as P

MESH = pl.DeviceIdType.MESH
CHEB_C = 8
FINE_LOW = 0.25
FINE_HIGH = 2.0
COARSE_LOW = 0.05
COARSE_HIGH = 2.0

FX0, FX1, FR0, FRN = 3, 7, 4, 32
CX0, CR0, CRN = 4, 4, 16
GUESS, DIFF, SOURCE, MASS = 0, 1, 2, 3

NEAR = [(i, j) for i in (-2, 2) for j in (-1, 1, 0)] + [(i, j) for i in (-1, 1) for j in (-1, 1)] + [(0, -1), (0, 1), (-1, 0), (1, 0)]
BESIDE = [o for o in NEAR if abs(o[0]) < 2]
LOW_Y, LOW_Z, LOW_X, ROOT = (0, 6), (1, 7), (2, 5), (3, 4)
C_SLOTS, A_SLOTS, B_SLOTS = 8, 2, 4
STEP, ITERATE = (0, 3), (1, 2)
RING = [(i, j) for i in (-1, 1) for j in (-1, 1)] + [(0, -1), (0, 1), (-1, 0), (1, 0)]


def cheb_coeffs(count_steps, low_end, high_end):
    center_val = (high_end + low_end) / 2.0
    half_width = (high_end - low_end) / 2.0
    sigma_val = center_val / half_width
    factor_prev = 1.0 / sigma_val
    coeffs_list = [(0.0, 1.0 / center_val)]
    for number in range(1, count_steps):
        factor_next = 1.0 / (2.0 * sigma_val - factor_prev)
        coeffs_list.append((factor_next * factor_prev, 2.0 * factor_next / half_width))
        factor_prev = factor_next
    return coeffs_list


def coarse_rows(os, width):
    if os == 1:
        return pl.ds(CR0 + CRN - width, width), pl.ds(CR0 - width, width)
    if os == -1:
        return pl.ds(CR0, width), pl.ds(CR0 + CRN, width)
    return pl.ds(CR0, CRN), pl.ds(CR0, CRN)


def coef_cut(o):
    return {2: (3, 5), -2: (0, 6)}.get(o[0], (0, C_SLOTS)) + (2 if abs(o[0]) == 2 else 4,)


def rhs_cut(o):
    if abs(o[0]) == 2 and o[1] != 0:
        return (1 if o[0] == 2 else 0), 1, 1
    return 0, A_SLOTS, (4 if o[0] == 0 else 3)


def iterate_cut(o):
    return {2: (1, 3), -2: (0, 3)}.get(o[0], (0, B_SLOTS)) + (2 if abs(o[0]) == 2 else 4,)


def fine_cut(o, start, size, width):
    if o == 1:
        return pl.ds(start + size - width, width), pl.ds(start - width, width)
    if o == -1:
        return pl.ds(start, width), pl.ds(start + size, width)
    return pl.ds(start, size), pl.ds(start, size)


def rim_messages():
    own_x, own_rows, all_four = pl.ds(FX0, 4), pl.ds(FR0, FRN), pl.ds(0, 4)
    beside = []
    for j in (-1, 1):
        beside.append(((0, j), all_four, own_x, own_x) + fine_cut(j, FR0, FRN, 3))
    for i in (-1, 1):
        for j in (-1, 1):
            beside.append(((i, j), all_four) + fine_cut(i, FX0, 4, 2) + fine_cut(j, FR0, FRN, 2))
    ranks = []
    for depth in range(3):
        arrays = all_four if depth < 2 else pl.ds(0, 2)
        ranks.append([
            ((-1, 0), arrays, pl.ds(FX0 + depth, 1), pl.ds(FX1 + depth, 1), own_rows, own_rows),
            ((1, 0), arrays, pl.ds(FX1 - 1 - depth, 1), pl.ds(FX0 - 1 - depth, 1), own_rows, own_rows)])
    return [beside] + ranks


def dot(a, b):
    bf16 = jnp.bfloat16
    high = a.astype(bf16)
    rest = a - high.astype(jnp.float32)
    middle = rest.astype(bf16)
    low = (rest - middle.astype(jnp.float32)).astype(bf16)
    parts = jnp.dot(jnp.concatenate([low, middle, high], 0), b.astype(bf16), preferred_element_type=jnp.float32)
    n = a.shape[0]
    return (parts[:n] + parts[n:2 * n]) + parts[2 * n:]


def kernel(source, guess, mass, diff, out, F, FX, FY, FZ, DIAG, INV, W1, W2, DIR, RES, L2, C, G, A, B, XA, XB, CD, SPREAD,
           load_sem, r_send, r_recv, c_send, c_recv, e_send, e_recv, b_send, b_recv, l_send, l_recv, ready):
    f32 = jnp.float32
    nbox, nsub = lax.axis_size("box"), lax.axis_size("sub")
    b, s = lax.axis_index("box"), lax.axis_index("sub")

    def both(p, q):
        return jnp.logical_and(p, q)

    def exists(o):
        box_in = {-2: b > 1, -1: b > 0, 0: None, 1: b < nbox - 1, 2: b < nbox - 2}[o[0]]
        sub_in = {-1: s > 0, 0: None, 1: s < nsub - 1}[o[1]]
        if box_in is None or sub_in is None:
            return sub_in if box_in is None else box_in
        return both(box_in, sub_in)

    inner = both(both(b > 1, b < nbox - 2), both(s > 0, s < nsub - 1))
    rim = jnp.logical_not(inner)

    def each(messages, act, back):
        @pl.when(inner)
        def _():
            for _, message in messages:
                act(message)

        @pl.when(rim)
        def _():
            for o, message in messages:
                pl.when(exists((-o[0], -o[1]) if back else o))(functools.partial(act, message))

    def start(messages):
        each(messages, lambda m: m.start(), False)

    def arrived(messages):
        each(messages, lambda m: m.wait_recv(), True)

    def left(messages):
        each(messages, lambda m: m.wait_send(), False)

    def message(o, src, dst, send, recv):
        return o, pltpu.make_async_remote_copy(
            src_ref=src, dst_ref=dst, send_sem=send, recv_sem=recv, device_id=(b + o[0], s + o[1]), device_id_type=MESH)

    barrier = pltpu.get_barrier_semaphore()

    def greet(o, semaphore):
        pl.semaphore_signal(semaphore, inc=1, device_id=(b + o[0], s + o[1]), device_id_type=MESH)

    def minus(o):
        return (-o[0], -o[1])

    origin = both(b == 0, s == 0)
    other = jnp.logical_not(origin)

    def is_origin(o):
        return both(b + o[0] == 0, s + o[1] == 0)

    def there(o):
        return both(exists(o), jnp.logical_not(is_origin(o)))

    n_sub = jnp.minimum(s, 1) + jnp.minimum(nsub - 1 - s, 1)
    n_beside = (jnp.minimum(b, 1) + jnp.minimum(nbox - 1 - b, 1) + 1) * (n_sub + 1) - 1
    n_near = (jnp.minimum(b, 2) + jnp.minimum(nbox - 1 - b, 2) + 1) * (n_sub + 1) - 1

    def wait_barrier(count):
        pl.when(count > 0)(lambda: pl.semaphore_wait(barrier, count))

    def slot(o):
        return ready.at[NEAR.index(o)]

    @pl.when(origin)
    def _():
        wait_barrier(n_near)
        for o in NEAR:
            if o[0] >= 0 and o[1] >= 0:
                pl.when(exists(o))(functools.partial(greet, o, slot(minus(o))))

    loads = []
    for k, ref in enumerate((guess, diff, source, mass)):
        for h in range(2):
            loads.append(pltpu.make_async_copy(
                ref.at[:, :, pl.ds(128 * h, 128)], F.at[k, pl.ds(FX0, 4), h, pl.ds(FR0, FRN)], load_sem.at[k, h]))
            loads[-1].start()
    for o in BESIDE:
        pl.when(both(exists(o), other))(functools.partial(greet, o, barrier))
    for o in NEAR:
        if abs(o[0]) == 2:
            pl.when(is_origin(o))(functools.partial(greet, o, barrier))
    def outside(x_cut, row_cut, X_cut, coarse_row_cut, n_x, n_rows, n_X, n_coarse_rows):
        F[0:3, x_cut, :, row_cut] = jnp.zeros((3, n_x, 2, n_rows, 128), f32)
        F[3:4, x_cut, :, row_cut] = jnp.ones((1, n_x, 2, n_rows, 128), f32)
        L2[x_cut, :, row_cut] = jnp.zeros((n_x, 2, n_rows, 128), f32)
        blank_coarse(X_cut, coarse_row_cut, n_X, n_coarse_rows)

    def blank_coarse(group_cut, row_cut, n_groups, n_rows):
        for ref, slots in ((C, C_SLOTS), (A, A_SLOTS), (B, B_SLOTS)):
            ref[group_cut, :, row_cut] = jnp.zeros((n_groups, slots, n_rows, 128), f32)

    def blank():
        every = slice(None)
        pl.when(b == 0)(lambda: outside(slice(0, FX0), every, slice(0, 2), every, FX0, 40, 2, 24))
        pl.when(b == nbox - 1)(lambda: outside(slice(FX1, 10), every, slice(3, 5), every, 10 - FX1, 40, 2, 24))
        pl.when(s == 0)(lambda: outside(every, slice(0, 4), every, slice(0, 4), 10, 4, 5, 4))
        pl.when(s == nsub - 1)(lambda: outside(every, slice(36, 40), every, slice(20, 24), 10, 4, 5, 4))
        pl.when(b == 1)(lambda: blank_coarse(slice(0, 1), every, 1, 24))
        pl.when(b == nbox - 2)(lambda: blank_coarse(slice(4, 5), every, 1, 24))

    first, k = [], 0
    for group in rim_messages():
        first.append([])
        for o, arrays, xs, xd, rs, rd in group:
            first[-1].append(message(o, F.at[arrays, xs, :, rs], F.at[arrays, xd, :, rd], r_send.at[k], r_recv.at[k]))
            k += 1
    flat = [m for group in first for m in group]
    by_origin = both(both(b < 2, s < 2), other)

    pl.when(by_origin)(lambda: wait_barrier(n_beside - 1))
    pl.when(jnp.logical_not(jnp.logical_or(origin, by_origin)))(lambda: wait_barrier(n_beside))

    for load in loads:
        load.wait()

    def send(o):
        for m in flat:
            if m[0] == o:
                m[1].start()

    def send_met(o):
        pl.semaphore_wait(slot(o), 1)
        send(o)

    @pl.when(inner)
    def _():
        for _, m in flat:
            m.start()

    @pl.when(rim)
    def _():
        for o in BESIDE:
            pl.when(there(o))(functools.partial(send, o))
        for o in BESIDE:
            if o[0] <= 0 and o[1] <= 0:
                pl.when(is_origin(o))(functools.partial(send_met, o))
    pl.when(rim)(blank)

    lane = lax.broadcasted_iota(jnp.int32, (256, 128), 0)
    cell = lax.broadcasted_iota(jnp.int32, (256, 128), 1)
    z_mean = jnp.where(lax.shift_right_logical(lane, 1) == cell, f32(0.5), f32(0.0))
    z_low = jnp.where(lax.shift_right_logical(lane + 1, 1) == cell, f32(0.5), f32(0.0))
    z_high = jnp.where(lax.shift_right_logical(lane + 1, 1) == cell + 1, f32(0.5), f32(0.0))
    row = lax.broadcasted_iota(jnp.int32, (2, 40, 128), 1)
    row_in = jnp.logical_and(jnp.logical_or(row >= FR0, s > 0), jnp.logical_or(row < FR0 + FRN, s < nsub - 1))
    row_mask = jnp.where(row_in, f32(1.0), f32(0.0))
    lane_f = lax.broadcasted_iota(jnp.int32, (2, 40, 128), 2)
    half = lax.broadcasted_iota(jnp.int32, (2, 40, 128), 0)
    z_first = jnp.logical_and(lane_f == 0, half == 0)
    z_last = jnp.logical_and(lane_f == 127, half == 1)

    def shift(v, edge, by):
        r = pltpu.roll(v, by, 2)
        return jnp.where(edge, jnp.stack([r[1], r[0]]), r)

    def from_below(v):
        return shift(v, lane_f == 0, 1)

    def from_above(v):
        return shift(v, lane_f == 127, 127)


    def slab_in(x):
        inside = jnp.logical_and(jnp.logical_or(x >= FX0, b > 0), jnp.logical_or(x < FX1, b < nbox - 1))
        return jnp.where(inside, f32(1.0), f32(0.0))

    def face(x):
        FX[x] = 0.5 * (F[DIFF, x - 1] + F[DIFF, x])

    def operator(x):
        d = F[DIFF, x]
        fy = 0.5 * (d + pltpu.roll(d, 1, 1))
        fz = 0.5 * (d + jnp.where(z_first, f32(0.0), from_below(d)))
        fz_high = 0.5 * (d + jnp.where(z_last, f32(0.0), from_above(d)))
        diag = F[MASS, x] + FX[x] + FX[x + 1] + fy + pltpu.roll(fy, 39, 1) + fz + fz_high
        FY[x] = fy
        FZ[x] = jnp.where(z_first, f32(0.0), fz)
        DIAG[x] = diag
        INV[x] = (row_mask * slab_in(x)) / diag

    def defect(u_ref, x):
        u = u_ref[x]
        fy, fz = FY[x], FZ[x]
        around = FX[x] * u_ref[x - 1] + FX[x + 1] * u_ref[x + 1]
        around = around + fy * pltpu.roll(u, 1, 1) + pltpu.roll(fy * u, 39, 1)
        around = around + fz * from_below(u) + from_above(fz * u)
        return (F[SOURCE, x] - DIAG[x] * u) + around, u

    fine = cheb_coeffs(2, FINE_LOW, FINE_HIGH)
    coarse = cheb_coeffs(CHEB_C, COARSE_LOW, COARSE_HIGH)

    def first_step(u_ref, to_ref, x):
        c, u = defect(u_ref, x)
        step_dir = (fine[0][1] * INV[x]) * c
        DIR[x] = step_dir
        to_ref[x] = u + step_dir

    def second_step(x):
        c, u = defect(W1, x)
        return u + (fine[1][0] * DIR[x] + (fine[1][1] * INV[x]) * c)

    def over(lo, hi, work, step=1):
        def turn(k, carry):
            work(lo + step * k)
            return carry

        lax.fori_loop(0, (hi - lo + step - 1) // step, turn, 0, unroll=True)

    def with_operator(x):
        operator(x)
        first_step(F.at[GUESS], W1, x)

    def smooth(x):
        W2[x] = second_step(x)

    def find_residual(x):
        RES[x] = defect(W2, x)[0]

    arrived(first[0])
    over(4, 7, face)
    arrived(first[1])
    def rows(ref, x, start):
        return ref[x, :, pl.ds(start, 16, 2), :]

    def wide(parts):
        return jnp.concatenate([jnp.concatenate([v[0], v[1]], 1) for v in parts], 0)


    D, M = F.at[DIFF], F.at[MASS]
    pair = {x: rows(D, x, FR0) + rows(D, x, FR0 + 1) for x in range(FX0 - 1, FX1 + 1)}
    low_y = {x: rows(D, x, FR0 - 1) + rows(D, x, FR0) for x in range(FX0, FX1)}
    high_y = {x: rows(D, x, FR0 + 1) + rows(D, x, FR0 + 2) for x in range(FX0, FX1)}
    in_mean, in_z = [], []
    for X in range(2):
        x = FX0 + 2 * X
        face_low, face_high = 0.25 * (pair[x - 1] + pair[x]), 0.25 * (pair[x + 1] + pair[x + 2])
        y_low, y_high = 0.25 * (low_y[x] + low_y[x + 1]), 0.25 * (high_y[x] + high_y[x + 1])
        mean_mass = 0.25 * (rows(M, x, FR0) + rows(M, x, FR0 + 1) + rows(M, x + 1, FR0) + rows(M, x + 1, FR0 + 1))
        in_mean += [face_low, y_low, mean_mass + 0.25 * (face_low + face_high + y_low + y_high)]
        in_z.append(0.25 * (pair[x] + pair[x + 1]))
    means = dot(wide(in_mean), z_mean)
    over_z = wide(in_z)
    lows_z, highs_z = dot(over_z, z_low), dot(over_z, z_high)
    own_s = []
    for X in range(2):
        fx, fy, d = (means[(3 * X + k) * 16:(3 * X + k + 1) * 16] for k in range(3))
        fz = lows_z[16 * X:16 * X + 16]
        d = d + 0.25 * (fz + highs_z[16 * X:16 * X + 16])
        sc = lax.rsqrt(d)
        sc = sc * (1.5 - 0.5 * d * sc * sc)
        own_s.append(sc)
        for kind, v in ((LOW_X, fx), (LOW_Y, fy), (LOW_Z, fz), (ROOT, sc)):
            C[2, kind[X], pl.ds(CR0, CRN), :] = v

    def coarse_messages(src, cut, sends, recvs):
        found = []
        for k, o in enumerate(NEAR):
            at, count, width = cut(o)
            rs, rd = coarse_rows(o[1], width)
            found.append(message(
                o, src.at[2, pl.ds(at, count), rs], src.at[2 - o[0], pl.ds(at, count), rd], sends.at[k], recvs.at[k]))
        start(found)
        return found

    def meet(o):
        pl.semaphore_wait(slot(o), 1)

    for o in ((-2, 0), (-2, -1)):
        pl.when(is_origin(o))(functools.partial(meet, o))
    coefs = coarse_messages(C, coef_cut, c_send, c_recv)

    over(3, 8, face, 4)
    over(3, 7, with_operator)
    arrived(first[2])
    over(2, 9, face, 6)
    over(2, 8, with_operator, 5)
    over(3, 7, smooth)
    arrived(first[3])
    over(1, 10, face, 8)
    over(1, 9, with_operator, 7)
    over(2, 8, smooth, 5)
    over(FX0, FX1, find_residual)

    means = []
    for X in range(2):
        x = FX0 + 2 * X
        means.append(0.25 * ((rows(RES, x, FR0) + rows(RES, x, FR0 + 1)) + (rows(RES, x + 1, FR0) + rows(RES, x + 1, FR0 + 1))))
    rhs = dot(wide(means), z_mean)
    for X in range(2):
        A[2, X, pl.ds(CR0, CRN), :] = own_s[X] * rhs[16 * X:16 * X + 16]
    e_one = coarse_messages(A, rhs_cut, e_send, e_recv)

    for x in range(FX0 - 1, FX1 + 1):
        L2[x, :, pl.ds(FR0, FRN), :] = W2[x, :, pl.ds(FR0, FRN), :]
    late = []
    for k, o in enumerate(RING):
        if o[1] == 0:
            at_x = FX1 - 2 if o[0] == 1 else FX0 + 1
            xs, xd = pl.ds(at_x, 1), pl.ds(at_x - 4 * o[0], 1)
        else:
            xs, xd = fine_cut(o[0], FX0, 4, 1)
        rs, rd = fine_cut(o[1], FR0, FRN, 2 if o[0] == 0 else 1)
        late.append(message(o, L2.at[xs, :, rs], L2.at[xd, :, rd], l_send.at[k], l_recv.at[k]))
    start(late)

    arrived(coefs)
    clane = lax.broadcasted_iota(jnp.int32, (24, 128), 1)

    def coef(kind, X):
        return C[X // 2, kind[X % 2]]

    for X in range(1, 10):
        sc = coef(ROOT, X)
        G[0, X] = coef(LOW_X, X) * ((0.25 * sc) * coef(ROOT, X - 1))
        if X < 9:
            low_row = coef(LOW_Y, X) * ((0.25 * sc) * pltpu.roll(sc, 1, 0))
            low_lane = jnp.where(clane == 0, f32(0.0), coef(LOW_Z, X) * ((0.25 * sc) * pltpu.roll(sc, 1, 1)))
            G[1, X], G[2, X] = low_row, low_lane
            G[3, X], G[4, X] = pltpu.roll(low_row, 23, 0), pltpu.roll(low_lane, 127, 1)

    def coarse_step(iterate, step_of, X, number):
        keep, gain = coarse[number]
        x = iterate(X)
        c = (A[X // 2, X % 2] - x) + G[0, X] * iterate(X - 1) + G[0, X + 1] * iterate(X + 1)
        along_y = G[1, X] * pltpu.roll(x, 1, 0) + G[3, X] * pltpu.roll(x, 23, 0)
        along_z = G[2, X] * pltpu.roll(x, 1, 1) + G[4, X] * pltpu.roll(x, 127, 1)
        c = c + (along_y + along_z)
        step_dir = keep * step_of(X) + gain * c
        return x + step_dir, step_dir

    left(flat)
    arrived(e_one)
    for X in range(10):
        begin = coarse[0][1] * A[X // 2, X % 2]
        XA[X] = begin
        CD[X] = begin

    def of(ref):
        return lambda X: ref[X]

    now, later = XA, XB
    for number in range(1, 4):
        for X in range(number, 10 - number):
            later[X], CD[X] = coarse_step(of(now), of(CD), X, number)
        now, later = later, now
    for X in range(CX0, CX0 + 2):
        new_x, new_d = coarse_step(of(now), of(CD), X, 4)
        B[2, ITERATE[X % 2], pl.ds(CR0, CRN), :] = new_x[CR0:CR0 + CRN]
        B[2, STEP[X % 2], pl.ds(CR0, CRN), :] = new_d[CR0:CR0 + CRN]
    e_two = coarse_messages(B, iterate_cut, b_send, b_recv)
    left(coefs + e_one)
    arrived(late)
    left(late)
    left(e_two)
    arrived(e_two)
    iterate, step_of = (lambda X: B[X // 2, ITERATE[X % 2]]), (lambda X: B[X // 2, STEP[X % 2]])
    for number, later in ((5, XA), (6, XB), (7, XA)):
        for X in range(number - 4, 14 - number):
            later[X], CD[X] = coarse_step(iterate, step_of, X, number)
        iterate, step_of = of(later), of(CD)

    spread_z = jnp.where(
        lax.shift_right_logical(lax.broadcasted_iota(jnp.int32, (128, 256), 1), 1) == lax.broadcasted_iota(jnp.int32, (128, 256), 0),
        f32(1.0), f32(0.0))
    corr = dot(jnp.concatenate([coef(ROOT, X) * iterate(X) for X in range(3, 7)], 0), spread_z)
    for X in range(4):
        for h in range(2):
            part = corr[24 * X:24 * X + 24, 128 * h:128 * h + 128]
            SPREAD[X, h, pl.ds(0, 24, 2), :] = part
            SPREAD[X, h, pl.ds(1, 24, 2), :] = part
    for x in range(1, 9):
        W2[x] = L2[x] + SPREAD[(x - 1) // 2, :, pl.ds(2 * CR0 - FR0, 40), :]

    over(2, 8, functools.partial(first_step, W2, W1))
    for x in range(FX0, FX1):
        last = second_step(x)
        for h in range(2):
            out[x - FX0, :, 128 * h:128 * h + 128] = last[h, FR0:FR0 + FRN]


def body(source, guess, mass_coef, diffusion):
    vmem = pltpu.VMEM
    fine_slabs = lambda: vmem((10, 2, 40, 128), jnp.float32)
    coarse_slabs = lambda: vmem((10, 24, 128), jnp.float32)
    n_rim, n_near, n_ring = sum(len(group) for group in rim_messages()), len(NEAR), len(RING)
    dma = pltpu.SemaphoreType.DMA
    return pl.pallas_call(
        kernel,
        out_shape=jax.ShapeDtypeStruct((4, 32, 256), jnp.float32),
        in_specs=[pl.BlockSpec(memory_space=pltpu.HBM)] * 4,
        out_specs=pl.BlockSpec(memory_space=pltpu.VMEM),
        scratch_shapes=[
            vmem((4, 10, 2, 40, 128), jnp.float32),
            fine_slabs(), fine_slabs(), fine_slabs(), fine_slabs(), fine_slabs(),
            fine_slabs(), fine_slabs(), fine_slabs(), fine_slabs(), fine_slabs(),
            vmem((5, C_SLOTS, 24, 128), jnp.float32),
            vmem((5, 10, 24, 128), jnp.float32),
            vmem((5, A_SLOTS, 24, 128), jnp.float32),
            vmem((5, B_SLOTS, 24, 128), jnp.float32),
            coarse_slabs(), coarse_slabs(), coarse_slabs(),
            vmem((4, 2, 48, 128), jnp.float32),
            dma((4, 2)),
            dma((n_rim,)), dma((n_rim,)),
            dma((n_near,)), dma((n_near,)),
            dma((n_near,)), dma((n_near,)),
            dma((n_near,)), dma((n_near,)),
            dma((n_ring,)), dma((n_ring,)),
            pltpu.SemaphoreType.REGULAR((len(NEAR),)),
        ],
        compiler_params=pltpu.CompilerParams(collective_id=0, has_side_effects=True, vmem_limit_bytes=48 * 2**20),
        name="cycle",
    )(*[pltpu.with_memory_space_constraint(v, pltpu.HBM) for v in (source, guess, mass_coef, diffusion)])


def solution(mesh):
    spec = P("box", "sub", None)
    return jax.shard_map(body, mesh=mesh, in_specs=(spec,) * 4, out_specs=spec, check_vma=False)
```
